128 devices in a mesh: rec: 4 (over x_lo, core), ch: 32 (over y, z, x_hi).
Axes of the slice: x: 4 (x_hi: 2, x_lo: 2; x = x_hi * 2 + x_lo), y: 4, z: 4, core: 2. Of those that a mesh axis runs over, the one named last changes fastest.
Arguments:
- samples: bfloat16 [4, 4, 1280, 6144], P('rec', None, 'ch')
- source_ids: int32 [8], replicated, may hold values from 0 to 5119
Outputs:
- correlations: float32 [8, 5120, 6144], P(None, ('rec', 'ch'))
The draws below stay inside these ranges and needn't reach their ends.
All inputs are finite; a program needn't handle non-finite values.
Results may differ from the reference program's by a relative error of at most 0.0003.
Values may be sent and summed in bfloat16 or wider, within the bound.
A program may use at most 128 MiB of HBM per device.

```python
import math
import jax
import jax.numpy as jnp
from jax import lax

NFFT = 6144
BAND = 64
NSRC = 8
NWIN = 4
SECT = 4
CH = 5120


def draw_samples(key, part):
    keys = jax.random.split(key, 5)
    shape = (NWIN, SECT, CH // SECT, NFFT)
    noise = jax.random.normal(keys[0], shape, jnp.float32)
    spread = math.log(10.0)
    scale = jnp.exp(jax.random.uniform(keys[1], (NWIN, SECT, CH // SECT, 1), jnp.float32, 0.0, spread))
    freqs = jax.random.randint(keys[2], (1, SECT, CH // SECT, 2), 1, NFFT // 2)
    amps = jax.random.uniform(keys[3], (1, SECT, CH // SECT, 2), jnp.float32, 0.5, 2.0)
    phases = jax.random.uniform(keys[4], (NWIN, SECT, CH // SECT, 2), jnp.float32, -math.pi, math.pi)
    moment = jnp.arange(NFFT, dtype=jnp.int32)
    first_turn = (freqs[..., 0:1] * moment % NFFT).astype(jnp.float32) * (2.0 * math.pi / NFFT)
    second_turn = (freqs[..., 1:2] * moment % NFFT).astype(jnp.float32) * (2.0 * math.pi / NFFT)
    tones = amps[..., 0:1] * jnp.cos(first_turn + phases[..., 0:1]) + amps[..., 1:2] * jnp.cos(second_turn + phases[..., 1:2])
    return (scale * (noise + tones)).astype(jnp.bfloat16)


def touch_ends(drawn, rng, smallest, high):
    dims = drawn.shape
    spot = [jax.random.randint(jax.random.fold_in(rng, axis), (), 0, dims[axis]) for axis in range(len(dims))]
    drawn = drawn.at[tuple(spot)].set(smallest)
    longest = dims.index(max(dims))
    spot[longest] = (spot[longest] + 1) % dims[longest]
    return drawn.at[tuple(spot)].set(high)


def setup_inputs(seed: int = 0) -> dict:
    key_list = jax.random.split(jax.random.key(seed), 3)
    return {
        "samples": draw_samples(jax.random.fold_in(key_list[2], 71), 0),
        "source_ids": touch_ends(jax.random.randint(key_list[1], (NSRC,), 0, CH), jax.random.fold_in(key_list[1], 1), 0, CH - 1).astype(jnp.int32),
    }


epsilon = 1e-06

def whiten(real_part, imag_part):
    energy = real_part * real_part + imag_part * imag_part
    leading = energy.shape[:-1]
    band_mean = lax.optimization_barrier(jnp.mean(energy.reshape(leading + (NFFT // BAND, BAND)), axis=-1, keepdims=True)) + epsilon
    factor = jnp.broadcast_to(lax.rsqrt(band_mean), leading + (NFFT // BAND, BAND)).reshape(leading + (NFFT,))
    return (real_part * factor, imag_part * factor)

def reference(samples, source_ids):
    section_len = CH // SECT
    source_section = (source_ids // section_len).astype(jnp.int32)
    source_offset = (source_ids % section_len).astype(jnp.int32)
    source_rows = samples[:, source_section, source_offset, :].astype(jnp.float32)
    source_spec = jnp.fft.fft(source_rows, axis=-1)
    source_real, source_imag = whiten(jnp.real(source_spec), jnp.imag(source_spec))

    def section(received):
        spec = jnp.fft.fft(received.astype(jnp.float32), axis=-1)
        white_real, white_imag = whiten(jnp.real(spec), jnp.imag(spec))
        cross_real = jnp.einsum('wsf,wcf->scf', source_real, white_real, precision=lax.Precision.HIGHEST)
        cross_real = cross_real + jnp.einsum('wsf,wcf->scf', source_imag, white_imag, precision=lax.Precision.HIGHEST)
        cross_imag = jnp.einsum('wsf,wcf->scf', source_imag, white_real, precision=lax.Precision.HIGHEST)
        cross_imag = cross_imag - jnp.einsum('wsf,wcf->scf', source_real, white_imag, precision=lax.Precision.HIGHEST)
        lagged = jnp.real(jnp.fft.ifft(cross_real + 1j * cross_imag, axis=-1)) * math.sqrt(NFFT / NWIN)
        return jnp.roll(lagged, NFFT // 2, axis=-1)
    stacked = lax.map(section, jnp.moveaxis(samples, 1, 0))
    return jnp.moveaxis(stacked, 0, 1).reshape(NSRC, CH, NFFT)
```

```python
import math
import numpy as np
import jax
import jax.numpy as jnp
from jax import lax
from jax.experimental import pallas as pl
from jax.experimental.pallas import tpu as pltpu
from jax.sharding import PartitionSpec as P

NFFT = 6144
SLOW = 48
FAST = 128
HALF = 25
NSRC = 8
NWIN = 4
EPS = 1e-06
ROWS = HALF * 16


def split_bf16(a):
    hi = a.astype(jnp.bfloat16)
    lo = (np.asarray(a, np.float32) - hi.astype(np.float32)).astype(jnp.bfloat16)
    return hi, lo


def tables():
    n = np.arange(FAST)
    ang = 2.0 * np.pi * ((n[:, None] * n[None, :]) % FAST) / FAST
    c, s = np.cos(ang), np.sin(ang)
    forward = np.block([[c, -s], [s, c]]).astype(np.float32)
    inverse = np.block([[c, s], [-s, c]]).astype(np.float32)
    fhi, flo = split_bf16(forward)
    ihi, ilo = split_bf16(inverse)
    fw = np.concatenate([fhi, flo], axis=0)
    iv = np.concatenate([ihi, ilo], axis=0)
    k1 = np.arange(HALF)[:, None]
    turn = 2.0 * np.pi * (k1 * n[None, :]) / NFFT
    scale = ((-1.0) ** k1) / math.sqrt(NWIN * NFFT) * np.where((k1 == 0) | (k1 == SLOW // 2), 1.0, 0.5)
    tw = np.stack([np.cos(turn), np.sin(turn), np.cos(turn) * scale, np.sin(turn) * scale], axis=1)
    tw = np.broadcast_to(tw[:, :, None, :], (HALF, 4, 8, FAST)).astype(np.float32)
    return fw, iv, np.ascontiguousarray(tw)


class V:
    def __init__(self, x, neg=False):
        self.x, self.neg = x, neg

    def __neg__(self):
        return V(self.x, not self.neg)

    def __add__(self, o):
        if self.neg == o.neg:
            return V(self.x + o.x, self.neg)
        return V(o.x - self.x) if self.neg else V(self.x - o.x)

    def __sub__(self, o):
        return self + (-o)

    def scale(self, f):
        if abs(f - 1.0) < 1e-12:
            return self
        return V(self.x * np.float32(abs(f)), self.neg != (f < 0))

    def get(self):
        return -self.x if self.neg else self.x


def turned(z, quarter, size):
    re, im = z
    step = (quarter * (16 // size)) % 16
    if step == 0:
        return z
    if step == 4:
        return im, -re
    if step == 12:
        return -im, re
    if step == 8:
        return -re, -im
    root = math.sqrt(0.5)
    if step == 2:
        return (re + im).scale(root), (im - re).scale(root)
    if step == 14:
        return (re - im).scale(root), (im + re).scale(root)
    c, s = math.cos(2 * math.pi * step / 16), math.sin(2 * math.pi * step / 16)
    return re.scale(c) + im.scale(s), im.scale(c) - re.scale(s)


def rfft(xs):
    n = len(xs)
    if n == 2:
        return [(xs[0] + xs[1], None), (xs[0] - xs[1], None)]
    even, odd = rfft(xs[0::2]), rfft(xs[1::2])
    out = [None] * (n // 2 + 1)
    out[0] = (even[0][0] + odd[0][0], None)
    out[n // 2] = (even[0][0] - odd[0][0], None)
    for k in range(1, n // 4):
        t = turned(odd[k], k, n)
        e = even[k]
        out[k] = (e[0] + t[0], e[1] + t[1])
        out[n // 2 - k] = (e[0] - t[0], t[1] - e[1])
    if n >= 4:
        k = n // 4
        out[k] = (even[k][0], -odd[k][0])
    return out


def irfft(zs):
    n = 2 * (len(zs) - 1)
    if n == 2:
        return [zs[0][0] + zs[1][0], zs[0][0] - zs[1][0]]
    even, odd = [None] * (n // 4 + 1), [None] * (n // 4 + 1)
    even[0] = (zs[0][0] + zs[n // 2][0], None)
    odd[0] = (zs[0][0] - zs[n // 2][0], None)
    for k in range(1, n // 4):
        a, b = zs[k], zs[n // 2 - k]
        even[k] = (a[0] + b[0], a[1] - b[1])
        odd[k] = turned((a[0] - b[0], a[1] + b[1]), n - k, n)
    k = n // 4
    even[k] = (zs[k][0].scale(2.0), None)
    odd[k] = (zs[k][1].scale(-2.0), None)
    xe, xo = irfft(even), irfft(odd)
    out = []
    for a, b in zip(xe, xo):
        out += [a, b]
    return out


R3 = math.sqrt(0.75)


def slow_forward(load):
    parts = []
    for a in range(3):
        parts.append(rfft([V(load((16 * a + 3 * b) % SLOW)) for b in range(16)]))
    out = [None] * HALF

    def put(c, d, z):
        k = next(k for k in range(SLOW) if k % 16 == c and k % 3 == d)
        if k <= SLOW // 2:
            out[k] = z
        elif out[SLOW - k] is None:
            out[SLOW - k] = (z[0], -z[1])

    for c in range(9):
        x, y, z = parts[0][c], parts[1][c], parts[2][c]
        if x[1] is None:
            t, s = y[0] + z[0], (y[0] - z[0]).scale(R3)
            put(c, 0, (x[0] + t, None))
            put(c, 1, (x[0] - t.scale(0.5), -s))
            continue
        tr, ti = y[0] + z[0], y[1] + z[1]
        sr, si = (y[0] - z[0]).scale(R3), (y[1] - z[1]).scale(R3)
        mr, mi = x[0] - tr.scale(0.5), x[1] - ti.scale(0.5)
        put(c, 0, (x[0] + tr, x[1] + ti))
        put(c, 1, (mr + si, mi - sr))
        put(c, 2, (mr - si, mi + sr))
    return out


def slow_inverse(bins):
    def get(c, d):
        k = next(k for k in range(SLOW) if k % 16 == c and k % 3 == d)
        if k <= SLOW // 2:
            return bins[k]
        z = bins[SLOW - k]
        return (z[0], -z[1])

    mid = [[None] * 9 for _ in range(3)]
    for c in range(9):
        x, y, z = get(c, 0), get(c, 1), get(c, 2)
        if c in (0, 8):
            tr, si = y[0], y[1].scale(2.0 * R3)
            m = x[0] - tr
            mid[0][c] = (x[0] + tr.scale(2.0), None)
            mid[1][c] = (m - si, None)
            mid[2][c] = (m + si, None)
            continue
        tr, ti = y[0] + z[0], y[1] + z[1]
        sr, si = (y[0] - z[0]).scale(R3), (y[1] - z[1]).scale(R3)
        mr, mi = x[0] - tr.scale(0.5), x[1] - ti.scale(0.5)
        mid[0][c] = (x[0] + tr, x[1] + ti)
        mid[1][c] = (mr - si, mi + sr)
        mid[2][c] = (mr + si, mi - sr)
    out = [None] * SLOW
    for a in range(3):
        xs = irfft(mid[a])
        for b in range(16):
            out[(16 * a + 3 * b) % SLOW] = xs[b]
    return out


def stack2(x):
    return jnp.concatenate([x, x], axis=0)


def put_split(hi_ref, lo_ref, k, re, im):
    rows = pl.ds(16 * k, 16)
    for half, x in ((0, re), (1, im)):
        hi = x.astype(jnp.bfloat16)
        lo = (x - hi.astype(jnp.float32)).astype(jnp.bfloat16)
        hi_ref[rows, pl.ds(FAST * half, FAST)] = hi
        lo_ref[rows, pl.ds(FAST * half, FAST)] = lo


def fast_dot(hi_ref, lo_ref, mat_ref, out_ref, pieces):
    step = ROWS // pieces
    for p in range(pieces):
        rows = pl.ds(p * step, step)
        hi, lo = hi_ref[rows, :], lo_ref[rows, :]
        mhi, mlo = mat_ref[0:256, :], mat_ref[256:512, :]
        acc = jnp.dot(hi, mhi, preferred_element_type=jnp.float32)
        acc = acc + jnp.dot(lo, mhi, preferred_element_type=jnp.float32)
        acc = acc + jnp.dot(hi, mlo, preferred_element_type=jnp.float32)
        out_ref[rows, :] = acc


def forward16(load, tw_ref, mat_ref, hi_ref, lo_ref, z_ref, pieces=1):
    bins = slow_forward(load)
    for k in range(HALF):
        re, im = bins[k]
        if k == 0:
            xr = re.get()
            put_split(hi_ref, lo_ref, 0, xr, jnp.zeros_like(xr))
            continue
        c, s = stack2(tw_ref[k, 0]), stack2(tw_ref[k, 1])
        if im is None:
            put_split(hi_ref, lo_ref, k, re.get() * c, -(re.get() * s))
            continue
        cr, ci = V(re.x * c, re.neg), V(im.x * c, im.neg)
        srr, sii = V(re.x * s, re.neg), V(im.x * s, im.neg)
        put_split(hi_ref, lo_ref, k, (cr + sii).get(), (ci - srr).get())
    fast_dot(hi_ref, lo_ref, mat_ref, z_ref, pieces)


def factors(z_ref, rows=16):
    def energy(k):
        re, im = z_ref[pl.ds(16 * k, 16), 0:128], z_ref[pl.ds(16 * k, 16), 128:256]
        return re * re + im * im

    def total(ks):
        es = [energy(k) for k in ks]
        while len(es) > 1:
            es = [es[i] + es[i + 1] if i + 1 < len(es) else es[i] for i in range(0, len(es), 2)]
        return es[0]

    low, high = total(range(1, 16)), total(range(17, 24))
    e16 = energy(16)
    lane = lax.broadcasted_iota(jnp.int32, (rows, FAST), 1)
    mirror = (FAST - 1) - lane

    def flip(x):
        return jnp.concatenate([
            jnp.take_along_axis(x[0:8], mirror[0:8], axis=1, mode="promise_in_bounds"),
            jnp.take_along_axis(x[8:16], mirror[8:16], axis=1, mode="promise_in_bounds"),
        ], axis=0)

    g0 = energy(0) + low
    g1 = e16 + high + energy(24) + flip(high)
    g2 = flip(low + e16)

    def nxt(x):
        return pltpu.roll(x, FAST - 1, 1)

    def prv(x):
        return pltpu.roll(x, 1, 1)

    g01, g12 = g0 + g1, g1 + g2
    g = g01 + g2
    ga = g + nxt(g0)
    gb_next, gb_prev = g12 + nxt(g01), g01 + prv(g12)
    gc = prv(g2) + g
    g0_at1 = prv(g) + g0
    g2_at2 = g2 + nxt(g)
    phase = lane % 4
    is0, is1, is2 = phase == 0, phase == 1, phase == 2
    l0 = jnp.where(is0, ga, jnp.where(is1, g0_at1, jnp.where(is2, gb_prev, gc)))
    l1 = jnp.where(is0, ga, jnp.where(is1, gb_next, jnp.where(is2, gb_prev, gc)))
    l2 = jnp.where(is0, ga, jnp.where(is1, gb_next, jnp.where(is2, g2_at2, gc)))
    f0, f1, f2 = [lax.rsqrt(l * np.float32(1.0 / 64) + np.float32(EPS)) for l in (l0, l1, l2)]
    return f0, f1, flip(f1), flip(f2)


def weights(fs, fx):
    p0, p1, q1, q2 = [a * b for a, b in zip(fs, fx)]
    return (p0, p0 + q2, p1 + q2, p1 + q1, p1)


def group_of(k):
    return 0 if k == 0 else 1 if k < 16 else 2 if k == 16 else 3 if k < 24 else 4


def cross_inverse(load_x, load_fx, load_s, load_fs, tw_ref, mat_ref, hi_ref, lo_ref, z_ref, store, pieces=1):
    hs = []
    for w in range(NWIN):
        fx = [stack2(f) for f in load_fx(w)]
        hs.append(weights(load_fs(w), fx))
    for k in range(HALF):
        cr = ci = None
        for w in range(NWIN):
            xr, xi = [stack2(x) for x in load_x(w, k)]
            sr, si = load_s(w, k)
            h = hs[w][group_of(k)]
            tr = (sr * xr + si * xi) * h
            ti = (si * xr - sr * xi) * h
            cr = tr if cr is None else cr + tr
            ci = ti if ci is None else ci + ti
        put_split(hi_ref, lo_ref, k, cr, ci)
    fast_dot(hi_ref, lo_ref, mat_ref, z_ref, pieces)
    bins = []
    for k in range(HALF):
        re, im = z_ref[pl.ds(16 * k, 16), 0:128], z_ref[pl.ds(16 * k, 16), 128:256]
        c, s = stack2(tw_ref[k, 2]), stack2(tw_ref[k, 3])
        real = re * c - im * s
        bins.append((V(real), None if k in (0, 24) else V(re * s + im * c)))
    for j, x in enumerate(slow_inverse(bins)):
        store(j, x.get())
def compute_kernel(x_ref, src_ref, fw_ref, iv_ref, tw_ref, out_ref, hi, lo, z, xs, fx, ss, fs, obuf, osem):
    def source_block(p, _):
        def load(n):
            return src_ref[pl.ds(pl.multiple_of(16 * p, 16), 16), pl.ds(FAST * n, FAST)].astype(jnp.float32)

        forward16(load, tw_ref, fw_ref, hi, lo, z)
        f = factors(z)
        for half in range(2):
            w = 2 * p + half
            for s in range(NSRC):
                row = 8 * half + s
                for i in range(4):
                    fs[w, s // 2, i, pl.ds(8 * (s % 2), 8), :] = jnp.broadcast_to(f[i][row : row + 1, :], (8, FAST))
                for k in range(HALF):
                    ss[w, s // 2, k, pl.ds(8 * (s % 2), 8), :] = jnp.broadcast_to(z[pl.ds(16 * k + row, 1), :], (8, 256))
        return 0

    lax.fori_loop(0, 2, source_block, 0)

    def keep(w, cb, half):
        for k in range(HALF):
            xs[w, cb, k] = z[pl.ds(16 * k + 8 * half, 8), :]

    def channel_block(i, _):
        w, p = i // 2, i % 2
        rows = pl.ds(pl.multiple_of(16 * p, 16), 16)

        def load(n):
            return x_ref[w, rows, pl.ds(FAST * n, FAST)].astype(jnp.float32)

        forward16(load, tw_ref, fw_ref, hi, lo, z)
        f = factors(z)
        for half in range(2):
            keep(w, 2 * p + half, half)
            for i in range(4):
                fx[w, 2 * p + half, i] = f[i][8 * half : 8 * half + 8, :]
        return 0

    lax.fori_loop(0, 8, channel_block, 0)

    def last_block(p, _):
        def load(n):
            return jnp.concatenate(
                [x_ref[2 * p + half, pl.ds(32, 8), pl.ds(FAST * n, FAST)].astype(jnp.float32) for half in range(2)], axis=0)

        forward16(load, tw_ref, fw_ref, hi, lo, z)
        f = factors(z)
        for half in range(2):
            keep(2 * p + half, 4, half)
            for i in range(4):
                fx[2 * p + half, 4, i] = f[i][8 * half : 8 * half + 8, :]
        return 0

    lax.fori_loop(0, 2, last_block, 0)

    def send(slot, cb, sp):
        return [pltpu.make_async_copy(
            obuf.at[slot, half],
            out_ref.at[2 * sp + half, pl.ds(pl.multiple_of(8 * cb, 8), 8), :],
            osem.at[slot, half]) for half in range(2)]

    def unit(u, _):
        cb, sp = u // 4, u % 4
        slot = u % 2

        @pl.when(u >= 2)
        def _():
            for c in send(slot, (u - 2) // 4, (u - 2) % 4):
                c.wait()

        def store(j, x):
            obuf[slot, 0, :, pl.ds(FAST * j, FAST)] = x[0:8]
            obuf[slot, 1, :, pl.ds(FAST * j, FAST)] = x[8:16]

        cross_inverse(
            lambda w, k: (xs[w, cb, k, :, 0:128], xs[w, cb, k, :, 128:256]),
            lambda w: [fx[w, cb, i] for i in range(4)],
            lambda w, k: (ss[w, sp, k, :, 0:128], ss[w, sp, k, :, 128:256]),
            lambda w: [fs[w, sp, i] for i in range(4)],
            tw_ref, iv_ref, hi, lo, z, store)
        for c in send(slot, cb, sp):
            c.start()
        return 0

    lax.fori_loop(0, 20, unit, 0)
    for u in (18, 19):
        for c in send(u % 2, u // 4, u % 4):
            c.wait()


def compute(x, src):
    fw, iv, tw = tables()
    vmem = pl.BlockSpec(memory_space=pltpu.VMEM)
    f32, bf16 = jnp.float32, jnp.bfloat16
    channels = x.shape[1]
    return pl.pallas_call(
        compute_kernel,
        out_shape=jax.ShapeDtypeStruct((NSRC, channels, NFFT), f32),
        in_specs=[vmem] * 5,
        out_specs=pl.BlockSpec(memory_space=pl.ANY),
        scratch_shapes=[
            pltpu.VMEM((ROWS, 256), bf16),
            pltpu.VMEM((ROWS, 256), bf16),
            pltpu.VMEM((ROWS, 256), f32),
            pltpu.VMEM((NWIN, 5, HALF, 8, 256), f32),
            pltpu.VMEM((NWIN, 5, 4, 8, FAST), f32),
            pltpu.VMEM((NWIN, 4, HALF, 16, 256), f32),
            pltpu.VMEM((NWIN, 4, 4, 16, FAST), f32),
            pltpu.VMEM((2, 2, 8, NFFT), f32),
            pltpu.SemaphoreType.DMA((2, 2)),
        ],
        compiler_params=pltpu.CompilerParams(vmem_limit_bytes=40 * 2**20),
    )(x, src, fw, iv, tw)


def shards(samples, source_ids):
    channels = samples.shape[2]
    section, line = lax.axis_index("rec"), lax.axis_index("ch")
    per_section = channels * 32
    ids = (jnp.arange(4, dtype=jnp.int32)[:, None] * per_section + line * channels + jnp.arange(channels, dtype=jnp.int32)[None, :]).reshape(-1)
    chooser = (source_ids[:, None] == ids[None, :]).astype(jnp.bfloat16)
    mine = jnp.dot(chooser, samples.reshape(4 * channels, NFFT), preferred_element_type=jnp.float32).astype(jnp.bfloat16)
    mine = lax.psum(mine, "ch")
    src = lax.all_gather(mine, "rec", axis=0).reshape(NWIN * NSRC, NFFT)
    x = lax.all_to_all(samples, "rec", split_axis=1, concat_axis=0, tiled=True)[:, 0]
    return compute(x, src)


def solution(mesh):
    return jax.shard_map(
        shards,
        mesh=mesh,
        in_specs=(P("rec", None, "ch", None), P()),
        out_specs=P(None, ("rec", "ch"), None),
        check_vma=False,
    )
```

```python
import math
import numpy as np
import jax
import jax.numpy as jnp
from jax import lax
from jax.experimental import pallas as pl
from jax.experimental.pallas import tpu as pltpu
from jax.sharding import PartitionSpec as P

NFFT = 6144
SLOW = 48
FAST = 128
HALF = 25
NSRC = 8
NWIN = 4
EPS = 1e-06
ROWS = HALF * 16


def split_bf16(a):
    hi = a.astype(jnp.bfloat16)
    lo = (np.asarray(a, np.float32) - hi.astype(np.float32)).astype(jnp.bfloat16)
    return hi, lo


def tables():
    n = np.arange(FAST)
    ang = 2.0 * np.pi * ((n[:, None] * n[None, :]) % FAST) / FAST
    c, s = np.cos(ang), np.sin(ang)
    forward = np.block([[c, -s], [s, c]]).astype(np.float32)
    inverse = np.block([[c, s], [-s, c]]).astype(np.float32)
    fhi, flo = split_bf16(forward)
    ihi, ilo = split_bf16(inverse)
    fw = np.concatenate([fhi, flo], axis=0)
    iv = np.concatenate([ihi, ilo], axis=0)
    k1 = np.arange(HALF)[:, None]
    turn = 2.0 * np.pi * (k1 * n[None, :]) / NFFT
    scale = ((-1.0) ** k1) / math.sqrt(NWIN * NFFT) * np.where((k1 == 0) | (k1 == SLOW // 2), 1.0, 0.5)
    tw = np.stack([np.cos(turn), np.sin(turn), np.cos(turn) * scale, np.sin(turn) * scale], axis=1)
    tw = np.broadcast_to(tw[:, :, None, :], (HALF, 4, 8, FAST)).astype(np.float32)
    return fw, iv, np.ascontiguousarray(tw)


class V:
    def __init__(self, x, neg=False):
        self.x, self.neg = x, neg

    def __neg__(self):
        return V(self.x, not self.neg)

    def __add__(self, o):
        if self.neg == o.neg:
            return V(self.x + o.x, self.neg)
        return V(o.x - self.x) if self.neg else V(self.x - o.x)

    def __sub__(self, o):
        return self + (-o)

    def scale(self, f):
        if abs(f - 1.0) < 1e-12:
            return self
        return V(self.x * np.float32(abs(f)), self.neg != (f < 0))

    def get(self):
        return -self.x if self.neg else self.x


def turned(z, quarter, size):
    re, im = z
    step = (quarter * (16 // size)) % 16
    if step == 0:
        return z
    if step == 4:
        return im, -re
    if step == 12:
        return -im, re
    if step == 8:
        return -re, -im
    root = math.sqrt(0.5)
    if step == 2:
        return (re + im).scale(root), (im - re).scale(root)
    if step == 14:
        return (re - im).scale(root), (im + re).scale(root)
    c, s = math.cos(2 * math.pi * step / 16), math.sin(2 * math.pi * step / 16)
    return re.scale(c) + im.scale(s), im.scale(c) - re.scale(s)


def rfft(xs):
    n = len(xs)
    if n == 2:
        return [(xs[0] + xs[1], None), (xs[0] - xs[1], None)]
    even, odd = rfft(xs[0::2]), rfft(xs[1::2])
    out = [None] * (n // 2 + 1)
    out[0] = (even[0][0] + odd[0][0], None)
    out[n // 2] = (even[0][0] - odd[0][0], None)
    for k in range(1, n // 4):
        t = turned(odd[k], k, n)
        e = even[k]
        out[k] = (e[0] + t[0], e[1] + t[1])
        out[n // 2 - k] = (e[0] - t[0], t[1] - e[1])
    if n >= 4:
        k = n // 4
        out[k] = (even[k][0], -odd[k][0])
    return out


def irfft(zs):
    n = 2 * (len(zs) - 1)
    if n == 2:
        return [zs[0][0] + zs[1][0], zs[0][0] - zs[1][0]]
    even, odd = [None] * (n // 4 + 1), [None] * (n // 4 + 1)
    even[0] = (zs[0][0] + zs[n // 2][0], None)
    odd[0] = (zs[0][0] - zs[n // 2][0], None)
    for k in range(1, n // 4):
        a, b = zs[k], zs[n // 2 - k]
        even[k] = (a[0] + b[0], a[1] - b[1])
        odd[k] = turned((a[0] - b[0], a[1] + b[1]), n - k, n)
    k = n // 4
    even[k] = (zs[k][0].scale(2.0), None)
    odd[k] = (zs[k][1].scale(-2.0), None)
    xe, xo = irfft(even), irfft(odd)
    out = []
    for a, b in zip(xe, xo):
        out += [a, b]
    return out


R3 = math.sqrt(0.75)


def slow_forward(load):
    parts = []
    for a in range(3):
        parts.append(rfft([V(load((16 * a + 3 * b) % SLOW)) for b in range(16)]))
    out = [None] * HALF

    def put(c, d, z):
        k = next(k for k in range(SLOW) if k % 16 == c and k % 3 == d)
        if k <= SLOW // 2:
            out[k] = z
        elif out[SLOW - k] is None:
            out[SLOW - k] = (z[0], -z[1])

    for c in range(9):
        x, y, z = parts[0][c], parts[1][c], parts[2][c]
        if x[1] is None:
            t, s = y[0] + z[0], (y[0] - z[0]).scale(R3)
            put(c, 0, (x[0] + t, None))
            put(c, 1, (x[0] - t.scale(0.5), -s))
            continue
        tr, ti = y[0] + z[0], y[1] + z[1]
        sr, si = (y[0] - z[0]).scale(R3), (y[1] - z[1]).scale(R3)
        mr, mi = x[0] - tr.scale(0.5), x[1] - ti.scale(0.5)
        put(c, 0, (x[0] + tr, x[1] + ti))
        put(c, 1, (mr + si, mi - sr))
        put(c, 2, (mr - si, mi + sr))
    return out


def slow_inverse(bins):
    def get(c, d):
        k = next(k for k in range(SLOW) if k % 16 == c and k % 3 == d)
        if k <= SLOW // 2:
            return bins[k]
        z = bins[SLOW - k]
        return (z[0], -z[1])

    mid = [[None] * 9 for _ in range(3)]
    for c in range(9):
        x, y, z = get(c, 0), get(c, 1), get(c, 2)
        if c in (0, 8):
            tr, si = y[0], y[1].scale(2.0 * R3)
            m = x[0] - tr
            mid[0][c] = (x[0] + tr.scale(2.0), None)
            mid[1][c] = (m - si, None)
            mid[2][c] = (m + si, None)
            continue
        tr, ti = y[0] + z[0], y[1] + z[1]
        sr, si = (y[0] - z[0]).scale(R3), (y[1] - z[1]).scale(R3)
        mr, mi = x[0] - tr.scale(0.5), x[1] - ti.scale(0.5)
        mid[0][c] = (x[0] + tr, x[1] + ti)
        mid[1][c] = (mr - si, mi + sr)
        mid[2][c] = (mr + si, mi - sr)
    out = [None] * SLOW
    for a in range(3):
        xs = irfft(mid[a])
        for b in range(16):
            out[(16 * a + 3 * b) % SLOW] = xs[b]
    return out


def stack2(x):
    return jnp.concatenate([x, x], axis=0)


def put(y_ref, k, re, im):
    rows = pl.ds(16 * k, 16)
    y_ref[rows, 0:128] = re
    y_ref[rows, 128:256] = im


def fast_dot(y_ref, mat_ref, out_ref):
    y = y_ref[...]
    hi = y.astype(jnp.bfloat16)
    lo = (y - hi.astype(jnp.float32)).astype(jnp.bfloat16)
    mats = jnp.concatenate([mat_ref[0:256, :], mat_ref[...]], axis=0)
    out_ref[...] = jnp.dot(jnp.concatenate([hi, lo, hi], axis=1), mats, preferred_element_type=jnp.float32)


def forward16(load, tw_ref, mat_ref, y_ref, z_ref):
    bins = slow_forward(load)
    for k in range(HALF):
        re, im = bins[k]
        if k == 0:
            xr = re.get()
            put(y_ref, 0, xr, jnp.zeros_like(xr))
            continue
        c, s = stack2(tw_ref[k, 0]), stack2(tw_ref[k, 1])
        if im is None:
            put(y_ref, k, re.get() * c, -(re.get() * s))
            continue
        cr, ci = V(re.x * c, re.neg), V(im.x * c, im.neg)
        srr, sii = V(re.x * s, re.neg), V(im.x * s, im.neg)
        put(y_ref, k, (cr + sii).get(), (ci - srr).get())
    fast_dot(y_ref, mat_ref, z_ref)


def factors(z_ref, rows=16):
    def energy(k):
        re, im = z_ref[pl.ds(16 * k, 16), 0:128], z_ref[pl.ds(16 * k, 16), 128:256]
        return re * re + im * im

    def total(ks):
        es = [energy(k) for k in ks]
        while len(es) > 1:
            es = [es[i] + es[i + 1] if i + 1 < len(es) else es[i] for i in range(0, len(es), 2)]
        return es[0]

    low, high = total(range(1, 16)), total(range(17, 24))
    e16 = energy(16)
    lane = lax.broadcasted_iota(jnp.int32, (rows, FAST), 1)
    mirror = (FAST - 1) - lane

    def flip(x):
        return jnp.concatenate([
            jnp.take_along_axis(x[0:8], mirror[0:8], axis=1, mode="promise_in_bounds"),
            jnp.take_along_axis(x[8:16], mirror[8:16], axis=1, mode="promise_in_bounds"),
        ], axis=0)

    g0 = energy(0) + low
    g1 = e16 + high + energy(24) + flip(high)
    g2 = flip(low + e16)

    def nxt(x):
        return pltpu.roll(x, FAST - 1, 1)

    def prv(x):
        return pltpu.roll(x, 1, 1)

    g01, g12 = g0 + g1, g1 + g2
    g = g01 + g2
    ga = g + nxt(g0)
    gb_next, gb_prev = g12 + nxt(g01), g01 + prv(g12)
    gc = prv(g2) + g
    g0_at1 = prv(g) + g0
    g2_at2 = g2 + nxt(g)
    phase = lane % 4
    is0, is1, is2 = phase == 0, phase == 1, phase == 2
    l0 = jnp.where(is0, ga, jnp.where(is1, g0_at1, jnp.where(is2, gb_prev, gc)))
    l1 = jnp.where(is0, ga, jnp.where(is1, gb_next, jnp.where(is2, gb_prev, gc)))
    l2 = jnp.where(is0, ga, jnp.where(is1, gb_next, jnp.where(is2, g2_at2, gc)))
    f0, f1, f2 = [lax.rsqrt(l * np.float32(1.0 / 64) + np.float32(EPS)) for l in (l0, l1, l2)]
    return f0, f1, flip(f1), flip(f2)


def weights(fs, fx):
    p0, p1, q1, q2 = [a * b for a, b in zip(fs, fx)]
    return (p0, p0 + q2, p1 + q2, p1 + q1, p1)


def group_of(k):
    return 0 if k == 0 else 1 if k < 16 else 2 if k == 16 else 3 if k < 24 else 4


def cross_inverse(load_x, load_fx, load_s, load_fs, tw_ref, mat_ref, y_ref, z_ref, store):
    hs = []
    for w in range(NWIN):
        fx = [stack2(f) for f in load_fx(w)]
        hs.append(weights(load_fs(w), fx))
    for k in range(HALF):
        cr = ci = None
        for w in range(NWIN):
            xr, xi = [stack2(x) for x in load_x(w, k)]
            sr, si = load_s(w, k)
            h = hs[w][group_of(k)]
            tr = (sr * xr + si * xi) * h
            ti = (si * xr - sr * xi) * h
            cr = tr if cr is None else cr + tr
            ci = ti if ci is None else ci + ti
        put(y_ref, k, cr, ci)
    fast_dot(y_ref, mat_ref, z_ref)
    bins = []
    for k in range(HALF):
        re, im = z_ref[pl.ds(16 * k, 16), 0:128], z_ref[pl.ds(16 * k, 16), 128:256]
        c, s = stack2(tw_ref[k, 2]), stack2(tw_ref[k, 3])
        real = re * c - im * s
        bins.append((V(real), None if k in (0, 24) else V(re * s + im * c)))
    for j, x in enumerate(slow_inverse(bins)):
        store(j, x.get())
GROUP = 16
LINE = 8
PIECE = NFFT // GROUP
CHUNKS = ((0, 16), (16, 16), (32, 8))
MESH = pl.DeviceIdType.MESH


def kernel(ids_ref, x_ref, flat_ref, fw_ref, iv_ref, tw_ref, out_ref,
           y, z, flat, recvx, part, recv1, recv2, srcs, xs, fx, ss, fs, obuf,
           flat_sem, own_sem, send_x, recv_x, send1, got1, send2, got2, send3, got3, osem):
    rec, ch = lax.axis_index("rec"), lax.axis_index("ch")
    q, x_hi = ch // 2, ch % 2
    line = x_hi * 4 + rec
    pair = rec // 2
    sibling = rec + 1 - 2 * (rec % 2)
    far = [(rec + 2) % 4, (sibling + 2) % 4]
    q_peer = [(q + i) % GROUP for i in range(1, GROUP)]
    q_id = [(rec, p * 2 + x_hi) for p in q_peer]
    l_peer = [(line + i) % LINE for i in range(1, LINE)]
    l_id = [(p % 4, q * 2 + p // 4) for p in l_peer]

    load_flat = pltpu.make_async_copy(flat_ref, flat, flat_sem)
    load_own = pltpu.make_async_copy(x_ref.at[rec], recvx.at[rec], own_sem)
    load_flat.start()
    load_own.start()
    barrier = pltpu.get_barrier_semaphore()
    for d in q_id + l_id:
        pl.semaphore_signal(barrier, inc=1, device_id=d, device_id_type=MESH)

    def move_x(n, peer, start, rows):
        return pltpu.make_async_remote_copy(
            src_ref=x_ref.at[peer, pl.ds(start, rows), :], dst_ref=recvx.at[rec, pl.ds(start, rows), :],
            send_sem=send_x.at[n], recv_sem=recv_x.at[n], device_id=(peer, ch), device_id_type=MESH)

    moves = []
    for c, (start, rows) in enumerate(CHUNKS):
        moves.append([move_x(2 * c + i, far[i], start, rows) for i in range(2)])
    near = move_x(6, sibling, 0, 40)

    row = lax.broadcasted_iota(jnp.int32, (NSRC, 160), 0)
    col = lax.broadcasted_iota(jnp.int32, (NSRC, 160), 1)
    ids = jnp.zeros((NSRC, 160), jnp.int32)
    for s in range(NSRC):
        ids = jnp.where(row == s, ids_ref[s], ids)
    here = (col // 40) * 1280 + ch * 40 + col % 40
    chooser = jnp.where(ids == here, 1.0, 0.0).astype(jnp.bfloat16)
    load_flat.wait()
    for j in range(GROUP):
        part[j] = jnp.dot(chooser, flat[:, pl.ds(PIECE * j, PIECE)], preferred_element_type=jnp.float32)
    recv1[q] = part[q]

    pl.semaphore_wait(barrier, GROUP - 1 + LINE - 1)

    for m in moves[0]:
        m.start()
    step1 = [pltpu.make_async_remote_copy(
        src_ref=part.at[p], dst_ref=recv1.at[q], send_sem=send1.at[i], recv_sem=got1.at[i],
        device_id=d, device_id_type=MESH) for i, (p, d) in enumerate(zip(q_peer, q_id))]
    for m in step1:
        m.start()
    near.start()
    for m in moves[1] + moves[2]:
        m.start()

    def keep(w, cb, half):
        for k in range(HALF):
            xs[w, cb, k] = z[pl.ds(16 * k + 8 * half, 8), :]

    def whole_block(w, p):
        rows = pl.ds(pl.multiple_of(16 * p, 16), 16)
        forward16(lambda n: recvx[w, rows, pl.ds(FAST * n, FAST)].astype(jnp.float32), tw_ref, fw_ref, y, z)
        f = factors(z)
        for half in range(2):
            keep(w, 2 * p + half, half)
            for i in range(4):
                fx[w, 2 * p + half, i] = f[i][8 * half : 8 * half + 8, :]

    def half_block(first):
        def load(n):
            return jnp.concatenate(
                [recvx[first + half, pl.ds(32, 8), pl.ds(FAST * n, FAST)].astype(jnp.float32) for half in range(2)], axis=0)

        forward16(load, tw_ref, fw_ref, y, z)
        f = factors(z)
        for half in range(2):
            keep(first + half, 4, half)
            for i in range(4):
                fx[first + half, 4, i] = f[i][8 * half : 8 * half + 8, :]

    load_own.wait()

    def own(p, _):
        whole_block(rec, p)
        return 0

    lax.fori_loop(0, 2, own, 0)

    for m in step1:
        m.wait()
    total = recv1[0]
    for j in range(1, GROUP):
        total = total + recv1[j]
    recv2[line] = total
    step2 = [pltpu.make_async_remote_copy(
        src_ref=recv2.at[line], dst_ref=recv2.at[line], send_sem=send2.at[i], recv_sem=got2.at[i],
        device_id=d, device_id_type=MESH) for i, d in enumerate(l_id)]
    for m in step2:
        m.start()

    near.wait()

    def second(p, _):
        whole_block(sibling, p)
        return 0

    lax.fori_loop(0, 2, second, 0)

    for m in step2:
        m.wait()
    srcs[q] = jnp.concatenate([recv2[w] + recv2[4 + w] for w in range(NWIN)], axis=0).astype(jnp.bfloat16)
    step3 = [pltpu.make_async_remote_copy(
        src_ref=srcs.at[q], dst_ref=srcs.at[q], send_sem=send3.at[i], recv_sem=got3.at[i],
        device_id=d, device_id_type=MESH) for i, d in enumerate(q_id)]
    for m in step3:
        m.start()
    half_block(2 * pair)
    for m in step3:
        m.wait()

    def source_block(p, _):
        rows = pl.ds(pl.multiple_of(16 * p, 16), 16)

        def load(n):
            return srcs[n // 3, rows, pl.ds(FAST * (n % 3), FAST)].astype(jnp.float32)

        forward16(load, tw_ref, fw_ref, y, z)
        f = factors(z)
        for half in range(2):
            w = 2 * p + half
            for s in range(NSRC):
                r = 8 * half + s
                for i in range(4):
                    fs[w, s // 2, i, pl.ds(8 * (s % 2), 8), :] = jnp.broadcast_to(f[i][r : r + 1, :], (8, FAST))
                for k in range(HALF):
                    ss[w, s // 2, k, pl.ds(8 * (s % 2), 8), :] = jnp.broadcast_to(z[pl.ds(16 * k + r, 1), :], (8, 256))
        return 0

    lax.fori_loop(0, 2, source_block, 0)

    def send(slot, cb, sp):
        return [pltpu.make_async_copy(
            obuf.at[slot, half],
            out_ref.at[2 * sp + half, pl.ds(pl.multiple_of(8 * cb, 8), 8), :],
            osem.at[slot, half]) for half in range(2)]

    def unit(u, _):
        cb, sp = u // 4, u % 4
        slot = u % 2

        @pl.when(u >= 2)
        def _():
            for c in send(slot, (u - 2) // 4, (u - 2) % 4):
                c.wait()

        def store(j, x):
            obuf[slot, 0, :, pl.ds(FAST * j, FAST)] = x[0:8]
            obuf[slot, 1, :, pl.ds(FAST * j, FAST)] = x[8:16]

        cross_inverse(
            lambda w, k: (xs[w, cb, k, :, 0:128], xs[w, cb, k, :, 128:256]),
            lambda w: [fx[w, cb, i] for i in range(4)],
            lambda w, k: (ss[w, sp, k, :, 0:128], ss[w, sp, k, :, 128:256]),
            lambda w: [fs[w, sp, i] for i in range(4)],
            tw_ref, iv_ref, y, z, store)
        for c in send(slot, cb, sp):
            c.start()
        return 0

    for c in range(2):
        for m in moves[c]:
            m.wait()

        def two(i, _):
            whole_block(2 * (1 - pair) + i, c)
            return 0

        lax.fori_loop(0, 2, two, 0)
        lax.fori_loop(8 * c, 8 * c + 8, unit, 0)

    for m in moves[2]:
        m.wait()
    half_block(2 * (1 - pair))
    lax.fori_loop(16, 20, unit, 0)
    for u in (18, 19):
        for c in send(u % 2, u // 4, u % 4):
            c.wait()


def shards(samples, source_ids):
    fw, iv, tw = tables()
    channels = samples.shape[2]
    vmem = pl.BlockSpec(memory_space=pltpu.VMEM)
    anywhere = pl.BlockSpec(memory_space=pl.ANY)
    f32, bf16 = jnp.float32, jnp.bfloat16
    dma = pltpu.SemaphoreType.DMA
    return pl.pallas_call(
        kernel,
        out_shape=jax.ShapeDtypeStruct((NSRC, channels, NFFT), f32),
        in_specs=[pl.BlockSpec(memory_space=pltpu.SMEM), anywhere, anywhere, vmem, vmem, vmem],
        out_specs=anywhere,
        scratch_shapes=[
            pltpu.VMEM((ROWS, 256), f32),
            pltpu.VMEM((ROWS, 256), f32),
            pltpu.VMEM((4 * channels, NFFT), bf16),
            pltpu.VMEM((NWIN, channels, NFFT), bf16),
            pltpu.VMEM((GROUP, NSRC, PIECE), f32),
            pltpu.VMEM((GROUP, NSRC, PIECE), f32),
            pltpu.VMEM((LINE, NSRC, PIECE), f32),
            pltpu.VMEM((GROUP, NWIN * NSRC, PIECE), bf16),
            pltpu.VMEM((NWIN, 5, HALF, 8, 256), f32),
            pltpu.VMEM((NWIN, 5, 4, 8, FAST), f32),
            pltpu.VMEM((NWIN, 4, HALF, 16, 256), f32),
            pltpu.VMEM((NWIN, 4, 4, 16, FAST), f32),
            pltpu.VMEM((2, 2, 8, NFFT), f32),
            dma, dma, dma((7,)), dma((7,)), dma((15,)), dma((15,)), dma((7,)), dma((7,)), dma((15,)), dma((15,)),
            dma((2, 2)),
        ],
        compiler_params=pltpu.CompilerParams(
            collective_id=0, has_side_effects=True, vmem_limit_bytes=48 * 2**20),
    )(source_ids, samples[0], samples.reshape(4 * channels, NFFT), fw, iv, tw)


def solution(mesh):
    return jax.shard_map(
        shards,
        mesh=mesh,
        in_specs=(P("rec", None, "ch", None), P()),
        out_specs=P(None, ("rec", "ch"), None),
        check_vma=False,
    )
```

```python
import math
import numpy as np
import jax
import jax.numpy as jnp
from jax import lax
from jax.experimental import pallas as pl
from jax.experimental.pallas import tpu as pltpu
from jax.sharding import PartitionSpec as P

NFFT = 6144
SLOW = 48
FAST = 128
HALF = 25
NSRC = 8
NWIN = 4
EPS = 1e-06
ROWS = HALF * 16


def split_bf16(a):
    hi = a.astype(jnp.bfloat16)
    lo = (np.asarray(a, np.float32) - hi.astype(np.float32)).astype(jnp.bfloat16)
    return hi, lo


def tables():
    n = np.arange(FAST)
    ang = 2.0 * np.pi * ((n[:, None] * n[None, :]) % FAST) / FAST
    c, s = np.cos(ang), np.sin(ang)
    forward = np.block([[c, -s], [s, c]]).astype(np.float32)
    inverse = np.block([[c, s], [-s, c]]).astype(np.float32)
    fhi, flo = split_bf16(forward)
    ihi, ilo = split_bf16(inverse)
    fw = np.concatenate([fhi, flo], axis=0)
    iv = np.concatenate([ihi, ilo], axis=0)
    k1 = np.arange(HALF)[:, None]
    turn = 2.0 * np.pi * (k1 * n[None, :]) / NFFT
    scale = ((-1.0) ** k1) / math.sqrt(NWIN * NFFT) * np.where((k1 == 0) | (k1 == SLOW // 2), 1.0, 0.5)
    tw = np.stack([np.cos(turn), np.sin(turn), np.cos(turn) * scale, np.sin(turn) * scale], axis=1)
    tw = np.broadcast_to(tw[:, :, None, :], (HALF, 4, 8, FAST)).astype(np.float32)
    return fw, iv, np.ascontiguousarray(tw)


class V:
    def __init__(self, x, neg=False):
        self.x, self.neg = x, neg

    def __neg__(self):
        return V(self.x, not self.neg)

    def __add__(self, o):
        if self.neg == o.neg:
            return V(self.x + o.x, self.neg)
        return V(o.x - self.x) if self.neg else V(self.x - o.x)

    def __sub__(self, o):
        return self + (-o)

    def scale(self, f):
        if abs(f - 1.0) < 1e-12:
            return self
        return V(self.x * np.float32(abs(f)), self.neg != (f < 0))

    def get(self):
        return -self.x if self.neg else self.x


def turned(z, quarter, size):
    re, im = z
    step = (quarter * (16 // size)) % 16
    if step == 0:
        return z
    if step == 4:
        return im, -re
    if step == 12:
        return -im, re
    if step == 8:
        return -re, -im
    root = math.sqrt(0.5)
    if step == 2:
        return (re + im).scale(root), (im - re).scale(root)
    if step == 14:
        return (re - im).scale(root), (im + re).scale(root)
    c, s = math.cos(2 * math.pi * step / 16), math.sin(2 * math.pi * step / 16)
    return re.scale(c) + im.scale(s), im.scale(c) - re.scale(s)


def rfft(xs):
    n = len(xs)
    if n == 2:
        return [(xs[0] + xs[1], None), (xs[0] - xs[1], None)]
    even, odd = rfft(xs[0::2]), rfft(xs[1::2])
    out = [None] * (n // 2 + 1)
    out[0] = (even[0][0] + odd[0][0], None)
    out[n // 2] = (even[0][0] - odd[0][0], None)
    for k in range(1, n // 4):
        t = turned(odd[k], k, n)
        e = even[k]
        out[k] = (e[0] + t[0], e[1] + t[1])
        out[n // 2 - k] = (e[0] - t[0], t[1] - e[1])
    if n >= 4:
        k = n // 4
        out[k] = (even[k][0], -odd[k][0])
    return out


def irfft(zs):
    n = 2 * (len(zs) - 1)
    if n == 2:
        return [zs[0][0] + zs[1][0], zs[0][0] - zs[1][0]]
    even, odd = [None] * (n // 4 + 1), [None] * (n // 4 + 1)
    even[0] = (zs[0][0] + zs[n // 2][0], None)
    odd[0] = (zs[0][0] - zs[n // 2][0], None)
    for k in range(1, n // 4):
        a, b = zs[k], zs[n // 2 - k]
        even[k] = (a[0] + b[0], a[1] - b[1])
        odd[k] = turned((a[0] - b[0], a[1] + b[1]), n - k, n)
    k = n // 4
    even[k] = (zs[k][0].scale(2.0), None)
    odd[k] = (zs[k][1].scale(-2.0), None)
    xe, xo = irfft(even), irfft(odd)
    out = []
    for a, b in zip(xe, xo):
        out += [a, b]
    return out


R3 = math.sqrt(0.75)


def slow_forward(load):
    parts = []
    for a in range(3):
        parts.append(rfft([V(load((16 * a + 3 * b) % SLOW)) for b in range(16)]))
    out = [None] * HALF

    def put(c, d, z):
        k = next(k for k in range(SLOW) if k % 16 == c and k % 3 == d)
        if k <= SLOW // 2:
            out[k] = z
        elif out[SLOW - k] is None:
            out[SLOW - k] = (z[0], -z[1])

    for c in range(9):
        x, y, z = parts[0][c], parts[1][c], parts[2][c]
        if x[1] is None:
            t, s = y[0] + z[0], (y[0] - z[0]).scale(R3)
            put(c, 0, (x[0] + t, None))
            put(c, 1, (x[0] - t.scale(0.5), -s))
            continue
        tr, ti = y[0] + z[0], y[1] + z[1]
        sr, si = (y[0] - z[0]).scale(R3), (y[1] - z[1]).scale(R3)
        mr, mi = x[0] - tr.scale(0.5), x[1] - ti.scale(0.5)
        put(c, 0, (x[0] + tr, x[1] + ti))
        put(c, 1, (mr + si, mi - sr))
        put(c, 2, (mr - si, mi + sr))
    return out


def slow_inverse(bins):
    def get(c, d):
        k = next(k for k in range(SLOW) if k % 16 == c and k % 3 == d)
        if k <= SLOW // 2:
            return bins[k]
        z = bins[SLOW - k]
        return (z[0], -z[1])

    mid = [[None] * 9 for _ in range(3)]
    for c in range(9):
        x, y, z = get(c, 0), get(c, 1), get(c, 2)
        if c in (0, 8):
            tr, si = y[0], y[1].scale(2.0 * R3)
            m = x[0] - tr
            mid[0][c] = (x[0] + tr.scale(2.0), None)
            mid[1][c] = (m - si, None)
            mid[2][c] = (m + si, None)
            continue
        tr, ti = y[0] + z[0], y[1] + z[1]
        sr, si = (y[0] - z[0]).scale(R3), (y[1] - z[1]).scale(R3)
        mr, mi = x[0] - tr.scale(0.5), x[1] - ti.scale(0.5)
        mid[0][c] = (x[0] + tr, x[1] + ti)
        mid[1][c] = (mr - si, mi + sr)
        mid[2][c] = (mr + si, mi - sr)
    out = [None] * SLOW
    for a in range(3):
        xs = irfft(mid[a])
        for b in range(16):
            out[(16 * a + 3 * b) % SLOW] = xs[b]
    return out


def stack2(x):
    return jnp.concatenate([x, x], axis=0)


def put(y_ref, k, re, im):
    rows = pl.ds(16 * k, 16)
    y_ref[rows, 0:128] = re
    y_ref[rows, 128:256] = im


def fast_dot(y_ref, mat_ref, out_ref):
    y = y_ref[...]
    hi = y.astype(jnp.bfloat16)
    lo = (y - hi.astype(jnp.float32)).astype(jnp.bfloat16)
    mats = jnp.concatenate([mat_ref[0:256, :], mat_ref[...]], axis=0)
    out_ref[...] = jnp.dot(jnp.concatenate([hi, lo, hi], axis=1), mats, preferred_element_type=jnp.float32)


def forward16(load, tw_ref, mat_ref, y_ref, z_ref):
    bins = slow_forward(load)
    for k in range(HALF):
        re, im = bins[k]
        if k == 0:
            xr = re.get()
            put(y_ref, 0, xr, jnp.zeros_like(xr))
            continue
        c, s = stack2(tw_ref[k, 0]), stack2(tw_ref[k, 1])
        if im is None:
            put(y_ref, k, re.get() * c, -(re.get() * s))
            continue
        cr, ci = V(re.x * c, re.neg), V(im.x * c, im.neg)
        srr, sii = V(re.x * s, re.neg), V(im.x * s, im.neg)
        put(y_ref, k, (cr + sii).get(), (ci - srr).get())
    fast_dot(y_ref, mat_ref, z_ref)


def factors(z_ref, rows=16):
    def energy(k):
        re, im = z_ref[pl.ds(16 * k, 16), 0:128], z_ref[pl.ds(16 * k, 16), 128:256]
        return re * re + im * im

    def total(ks):
        es = [energy(k) for k in ks]
        while len(es) > 1:
            es = [es[i] + es[i + 1] if i + 1 < len(es) else es[i] for i in range(0, len(es), 2)]
        return es[0]

    low, high = total(range(1, 16)), total(range(17, 24))
    e16 = energy(16)
    lane = lax.broadcasted_iota(jnp.int32, (rows, FAST), 1)
    mirror = (FAST - 1) - lane

    def flip(x):
        return jnp.concatenate([
            jnp.take_along_axis(x[0:8], mirror[0:8], axis=1, mode="promise_in_bounds"),
            jnp.take_along_axis(x[8:16], mirror[8:16], axis=1, mode="promise_in_bounds"),
        ], axis=0)

    g0 = energy(0) + low
    g1 = e16 + high + energy(24) + flip(high)
    g2 = flip(low + e16)

    def nxt(x):
        return pltpu.roll(x, FAST - 1, 1)

    def prv(x):
        return pltpu.roll(x, 1, 1)

    g01, g12 = g0 + g1, g1 + g2
    g = g01 + g2
    ga = g + nxt(g0)
    gb_next, gb_prev = g12 + nxt(g01), g01 + prv(g12)
    gc = prv(g2) + g
    g0_at1 = prv(g) + g0
    g2_at2 = g2 + nxt(g)
    phase = lane % 4
    is0, is1, is2 = phase == 0, phase == 1, phase == 2
    l0 = jnp.where(is0, ga, jnp.where(is1, g0_at1, jnp.where(is2, gb_prev, gc)))
    l1 = jnp.where(is0, ga, jnp.where(is1, gb_next, jnp.where(is2, gb_prev, gc)))
    l2 = jnp.where(is0, ga, jnp.where(is1, gb_next, jnp.where(is2, g2_at2, gc)))
    f0, f1, f2 = [lax.rsqrt(l * np.float32(1.0 / 64) + np.float32(EPS)) for l in (l0, l1, l2)]
    return f0, f1, flip(f1), flip(f2)


def weights(fs, fx):
    p0, p1, q1, q2 = [a * b for a, b in zip(fs, fx)]
    return (p0, p0 + q2, p1 + q2, p1 + q1, p1)


def group_of(k):
    return 0 if k == 0 else 1 if k < 16 else 2 if k == 16 else 3 if k < 24 else 4


def cross_inverse(load_x, load_fx, load_s, load_fs, tw_ref, mat_ref, y_ref, z_ref, store):
    hs = []
    for w in range(NWIN):
        fx = [stack2(f) for f in load_fx(w)]
        hs.append(weights(load_fs(w), fx))
    for k in range(HALF):
        cr = ci = None
        for w in range(NWIN):
            xr, xi = [stack2(x) for x in load_x(w, k)]
            sr, si = load_s(w, k)
            h = hs[w][group_of(k)]
            tr = (sr * xr + si * xi) * h
            ti = (si * xr - sr * xi) * h
            cr = tr if cr is None else cr + tr
            ci = ti if ci is None else ci + ti
        put(y_ref, k, cr, ci)
    fast_dot(y_ref, mat_ref, z_ref)
    bins = []
    for k in range(HALF):
        re, im = z_ref[pl.ds(16 * k, 16), 0:128], z_ref[pl.ds(16 * k, 16), 128:256]
        c, s = stack2(tw_ref[k, 0]), stack2(tw_ref[k, 1])
        real = re * c - im * s
        bins.append((V(real), None if k in (0, 24) else V(re * s + im * c)))
    for j, x in enumerate(slow_inverse(bins)):
        store(j, x.get())
GROUP = 16
LINE = 8
PIECE = NFFT // GROUP
CHUNKS = ((0, 16), (16, 16), (32, 8))
MESH = pl.DeviceIdType.MESH


def gather_kernel(ids_hbm, x_ref, flat_ref, fw_hbm, tw_hbm, iv_hbm, it_hbm, xs, fx, ss, fs, iv_ref, it_ref,
                  ids_ref, fw_ref, tw_ref, y, z, flat, recvx, part, recv1, recv2, srcs,
                  load_sem, flat_sem, own_sem, send_x, recv_x, send1, got1, send2, got2, send3, got3):
    rec, ch = lax.axis_index("rec"), lax.axis_index("ch")
    q, x_hi = ch // 2, ch % 2
    line = x_hi * 4 + rec
    pair = rec // 2
    sibling = rec + 1 - 2 * (rec % 2)
    far = [(rec + 2) % 4, (sibling + 2) % 4]
    q_peer = [(q + i) % GROUP for i in range(1, GROUP)]
    q_id = [(rec, p * 2 + x_hi) for p in q_peer]
    l_peer = [(line + i) % LINE for i in range(1, LINE)]
    l_id = [(p % 4, q * 2 + p // 4) for p in l_peer]

    load_ids = pltpu.make_async_copy(ids_hbm, ids_ref, load_sem.at[0])
    load_flat = pltpu.make_async_copy(flat_ref, flat, flat_sem)
    load_fw = pltpu.make_async_copy(fw_hbm, fw_ref, load_sem.at[1])
    load_tw = pltpu.make_async_copy(tw_hbm, tw_ref, load_sem.at[2])
    load_own = pltpu.make_async_copy(x_ref.at[rec], recvx.at[rec], own_sem)
    load_iv = pltpu.make_async_copy(iv_hbm, iv_ref, load_sem.at[3])
    load_it = pltpu.make_async_copy(it_hbm, it_ref, load_sem.at[4])
    for m in (load_ids, load_flat, load_fw, load_tw, load_own, load_iv, load_it):
        m.start()
    barrier = pltpu.get_barrier_semaphore()
    for d in q_id + l_id:
        pl.semaphore_signal(barrier, inc=1, device_id=d, device_id_type=MESH)

    def move_x(n, peer, start, rows):
        return pltpu.make_async_remote_copy(
            src_ref=x_ref.at[peer, pl.ds(start, rows), :], dst_ref=recvx.at[rec, pl.ds(start, rows), :],
            send_sem=send_x.at[n], recv_sem=recv_x.at[n], device_id=(peer, ch), device_id_type=MESH)

    moves = []
    for c, (start, rows) in enumerate(CHUNKS):
        moves.append([move_x(2 * c + i, far[i], start, rows) for i in range(2)])
    near = move_x(6, sibling, 0, 40)

    load_ids.wait()
    row = lax.broadcasted_iota(jnp.int32, (NSRC, 160), 0)
    col = lax.broadcasted_iota(jnp.int32, (NSRC, 160), 1)
    ids = jnp.zeros((NSRC, 160), jnp.int32)
    for s in range(NSRC):
        ids = jnp.where(row == s, ids_ref[s], ids)
    here = (col // 40) * 1280 + ch * 40 + col % 40
    chooser = jnp.where(ids == here, 1.0, 0.0).astype(jnp.bfloat16)
    load_flat.wait()
    for j in range(GROUP):
        part[j] = jnp.dot(chooser, flat[:, pl.ds(PIECE * j, PIECE)], preferred_element_type=jnp.float32)
    recv1[q] = part[q]

    pl.semaphore_wait(barrier, GROUP - 1 + LINE - 1)

    for m in moves[0]:
        m.start()
    step1 = [pltpu.make_async_remote_copy(
        src_ref=part.at[p], dst_ref=recv1.at[q], send_sem=send1.at[i], recv_sem=got1.at[i],
        device_id=d, device_id_type=MESH) for i, (p, d) in enumerate(zip(q_peer, q_id))]
    for m in step1:
        m.start()
    near.start()

    def keep(w, cb, half):
        for k in range(HALF):
            xs[w, cb, k] = z[pl.ds(16 * k + 8 * half, 8), :]

    def whole_block(w, p):
        rows = pl.ds(pl.multiple_of(16 * p, 16), 16)
        forward16(lambda n: recvx[w, rows, pl.ds(FAST * n, FAST)].astype(jnp.float32), tw_ref, fw_ref, y, z)
        f = factors(z)
        for half in range(2):
            keep(w, 2 * p + half, half)
            for i in range(4):
                fx[w, 2 * p + half, i] = f[i][8 * half : 8 * half + 8, :]

    def half_block(first):
        def load(n):
            return jnp.concatenate(
                [recvx[first + half, pl.ds(32, 8), pl.ds(FAST * n, FAST)].astype(jnp.float32) for half in range(2)], axis=0)

        forward16(load, tw_ref, fw_ref, y, z)
        f = factors(z)
        for half in range(2):
            keep(first + half, 4, half)
            for i in range(4):
                fx[first + half, 4, i] = f[i][8 * half : 8 * half + 8, :]

    for m in (load_fw, load_tw, load_own, load_iv, load_it):
        m.wait()

    def own(p, _):
        whole_block(rec, p)
        return 0

    lax.fori_loop(0, 2, own, 0)

    for m in step1:
        m.wait()
    total = recv1[0]
    for j in range(1, GROUP):
        total = total + recv1[j]
    recv2[line] = total
    step2 = [pltpu.make_async_remote_copy(
        src_ref=recv2.at[line], dst_ref=recv2.at[line], send_sem=send2.at[i], recv_sem=got2.at[i],
        device_id=d, device_id_type=MESH) for i, d in enumerate(l_id)]
    for m in step2 + moves[1] + moves[2]:
        m.start()

    near.wait()

    def second(p, _):
        whole_block(sibling, p)
        return 0

    lax.fori_loop(0, 2, second, 0)

    for m in step2:
        m.wait()
    srcs[q] = jnp.concatenate([recv2[w] + recv2[4 + w] for w in range(NWIN)], axis=0).astype(jnp.bfloat16)
    step3 = [pltpu.make_async_remote_copy(
        src_ref=srcs.at[q], dst_ref=srcs.at[q], send_sem=send3.at[i], recv_sem=got3.at[i],
        device_id=d, device_id_type=MESH) for i, d in enumerate(q_id)]
    for m in step3:
        m.start()
    half_block(2 * pair)
    for m in step3:
        m.wait()

    def source_block(p, _):
        rows = pl.ds(pl.multiple_of(16 * p, 16), 16)

        def load(n):
            return srcs[n // 3, rows, pl.ds(FAST * (n % 3), FAST)].astype(jnp.float32)

        forward16(load, tw_ref, fw_ref, y, z)
        f = factors(z)
        for half in range(2):
            w = 2 * p + half
            for s in range(NSRC):
                r = 8 * half + s
                for i in range(4):
                    fs[w, s // 2, i, pl.ds(8 * (s % 2), 8), :] = jnp.broadcast_to(f[i][r : r + 1, :], (8, FAST))
                for k in range(HALF):
                    ss[w, s // 2, k, pl.ds(8 * (s % 2), 8), :] = jnp.broadcast_to(z[pl.ds(16 * k + r, 1), :], (8, 256))
        return 0

    lax.fori_loop(0, 2, source_block, 0)

    for c in range(2):
        for m in moves[c]:
            m.wait()

        def two(i, _):
            whole_block(2 * (1 - pair) + i, c)
            return 0

        lax.fori_loop(0, 2, two, 0)

    for m in moves[2]:
        m.wait()
    half_block(2 * (1 - pair))


def correlate_kernel(xs, fx, ss, fs, iv_ref, tw_ref, out_ref, y, z, obuf, osem):
    def send(slot, cb, sp):
        return [pltpu.make_async_copy(
            obuf.at[slot, half],
            out_ref.at[2 * sp + half, pl.ds(pl.multiple_of(8 * cb, 8), 8), :],
            osem.at[slot, half]) for half in range(2)]

    def unit(u, _):
        cb, sp = u // 4, u % 4
        slot = u % 2

        @pl.when(u >= 2)
        def _():
            for c in send(slot, (u - 2) // 4, (u - 2) % 4):
                c.wait()

        def store(j, x):
            obuf[slot, 0, :, pl.ds(FAST * j, FAST)] = x[0:8]
            obuf[slot, 1, :, pl.ds(FAST * j, FAST)] = x[8:16]

        cross_inverse(
            lambda w, k: (xs[w, cb, k, :, 0:128], xs[w, cb, k, :, 128:256]),
            lambda w: [fx[w, cb, i] for i in range(4)],
            lambda w, k: (ss[w, sp, k, :, 0:128], ss[w, sp, k, :, 128:256]),
            lambda w: [fs[w, sp, i] for i in range(4)],
            tw_ref, iv_ref, y, z, store)
        for c in send(slot, cb, sp):
            c.start()
        return 0

    lax.fori_loop(0, 20, unit, 0)
    for u in (18, 19):
        for c in send(u % 2, u // 4, u % 4):
            c.wait()


def shards(samples, source_ids):
    fw, iv, tw = tables()
    channels = samples.shape[2]
    vmem = pl.BlockSpec(memory_space=pltpu.VMEM)
    hbm = pl.BlockSpec(memory_space=pltpu.HBM)
    f32, bf16 = jnp.float32, jnp.bfloat16
    dma = pltpu.SemaphoreType.DMA
    twist, square = pltpu.VMEM((HALF, 2, 8, FAST), f32), pltpu.VMEM((512, 256), bf16)
    spectra = pl.pallas_call(
        gather_kernel,
        out_shape=[
            jax.ShapeDtypeStruct((NWIN, 5, HALF, 8, 256), f32),
            jax.ShapeDtypeStruct((NWIN, 5, 4, 8, FAST), f32),
            jax.ShapeDtypeStruct((NWIN, 4, HALF, 16, 256), f32),
            jax.ShapeDtypeStruct((NWIN, 4, 4, 16, FAST), f32),
            jax.ShapeDtypeStruct((512, 256), bf16),
            jax.ShapeDtypeStruct((HALF, 2, 8, FAST), f32),
        ],
        in_specs=[hbm] * 7,
        out_specs=[vmem] * 6,
        scratch_shapes=[
            pltpu.SMEM((NSRC,), jnp.int32),
            square,
            twist,
            pltpu.VMEM((ROWS, 256), f32),
            pltpu.VMEM((ROWS, 256), f32),
            pltpu.VMEM((4 * channels, NFFT), bf16),
            pltpu.VMEM((NWIN, channels, NFFT), bf16),
            pltpu.VMEM((GROUP, NSRC, PIECE), f32),
            pltpu.VMEM((GROUP, NSRC, PIECE), f32),
            pltpu.VMEM((LINE, NSRC, PIECE), f32),
            pltpu.VMEM((GROUP, NWIN * NSRC, PIECE), bf16),
            dma((5,)), dma, dma, dma((7,)), dma((7,)), dma((15,)), dma((15,)), dma((7,)), dma((7,)), dma((15,)), dma((15,)),
        ],
        compiler_params=pltpu.CompilerParams(
            collective_id=0, has_side_effects=True, vmem_limit_bytes=32 * 2**20),
    )(*[pltpu.with_memory_space_constraint(jnp.asarray(a), pltpu.HBM) for a in (
        source_ids, samples[0], samples.reshape(4 * channels, NFFT), fw, tw[:, 0:2], iv, tw[:, 2:4])])
    return pl.pallas_call(
        correlate_kernel,
        out_shape=jax.ShapeDtypeStruct((NSRC, channels, NFFT), f32),
        in_specs=[vmem] * 6,
        out_specs=hbm,
        scratch_shapes=[
            pltpu.VMEM((ROWS, 256), f32),
            pltpu.VMEM((ROWS, 256), f32),
            pltpu.VMEM((2, 2, 8, NFFT), f32),
            dma((2, 2)),
        ],
        compiler_params=pltpu.CompilerParams(vmem_limit_bytes=32 * 2**20),
    )(*spectra)


def solution(mesh):
    return jax.shard_map(
        shards,
        mesh=mesh,
        in_specs=(P("rec", None, "ch", None), P()),
        out_specs=P(None, ("rec", "ch"), None),
        check_vma=False,
    )
```

```python
import math
import numpy as np
import jax
import jax.numpy as jnp
from jax import lax
from jax.experimental import pallas as pl
from jax.experimental.pallas import tpu as pltpu
from jax.sharding import PartitionSpec as P

NFFT = 6144
SLOW = 48
FAST = 128
HALF = 25
NSRC = 8
NWIN = 4
EPS = 1e-06
ROWS = HALF * 16


def split_bf16(a):
    hi = a.astype(jnp.bfloat16)
    lo = (np.asarray(a, np.float32) - hi.astype(np.float32)).astype(jnp.bfloat16)
    return hi, lo


def tables():
    n = np.arange(FAST)
    ang = 2.0 * np.pi * ((n[:, None] * n[None, :]) % FAST) / FAST
    c, s = np.cos(ang), np.sin(ang)
    forward = np.block([[c, -s], [s, c]]).astype(np.float32)
    inverse = np.block([[c, s], [-s, c]]).astype(np.float32)
    fhi, flo = split_bf16(forward)
    ihi, ilo = split_bf16(inverse)
    fw = np.concatenate([fhi, flo], axis=0)
    iv = np.concatenate([ihi, ilo], axis=0)
    k1 = np.arange(HALF)[:, None]
    turn = 2.0 * np.pi * (k1 * n[None, :]) / NFFT
    scale = ((-1.0) ** k1) / math.sqrt(NWIN * NFFT) * np.where((k1 == 0) | (k1 == SLOW // 2), 1.0, 0.5)
    tw = np.stack([np.cos(turn), np.sin(turn), np.cos(turn) * scale, np.sin(turn) * scale], axis=1)
    tw = np.broadcast_to(tw[:, :, None, :], (HALF, 4, 8, FAST)).astype(np.float32)
    return fw, iv, np.ascontiguousarray(tw)


class V:
    def __init__(self, x, neg=False):
        self.x, self.neg = x, neg

    def __neg__(self):
        return V(self.x, not self.neg)

    def __add__(self, o):
        if self.neg == o.neg:
            return V(self.x + o.x, self.neg)
        return V(o.x - self.x) if self.neg else V(self.x - o.x)

    def __sub__(self, o):
        return self + (-o)

    def scale(self, f):
        if abs(f - 1.0) < 1e-12:
            return self
        return V(self.x * np.float32(abs(f)), self.neg != (f < 0))

    def get(self):
        return -self.x if self.neg else self.x


def turned(z, quarter, size):
    re, im = z
    step = (quarter * (16 // size)) % 16
    if step == 0:
        return z
    if step == 4:
        return im, -re
    if step == 12:
        return -im, re
    if step == 8:
        return -re, -im
    root = math.sqrt(0.5)
    if step == 2:
        return (re + im).scale(root), (im - re).scale(root)
    if step == 14:
        return (re - im).scale(root), (im + re).scale(root)
    c, s = math.cos(2 * math.pi * step / 16), math.sin(2 * math.pi * step / 16)
    return re.scale(c) + im.scale(s), im.scale(c) - re.scale(s)


def rfft(xs):
    n = len(xs)
    if n == 2:
        return [(xs[0] + xs[1], None), (xs[0] - xs[1], None)]
    even, odd = rfft(xs[0::2]), rfft(xs[1::2])
    out = [None] * (n // 2 + 1)
    out[0] = (even[0][0] + odd[0][0], None)
    out[n // 2] = (even[0][0] - odd[0][0], None)
    for k in range(1, n // 4):
        t = turned(odd[k], k, n)
        e = even[k]
        out[k] = (e[0] + t[0], e[1] + t[1])
        out[n // 2 - k] = (e[0] - t[0], t[1] - e[1])
    if n >= 4:
        k = n // 4
        out[k] = (even[k][0], -odd[k][0])
    return out


def irfft(zs):
    n = 2 * (len(zs) - 1)
    if n == 2:
        return [zs[0][0] + zs[1][0], zs[0][0] - zs[1][0]]
    even, odd = [None] * (n // 4 + 1), [None] * (n // 4 + 1)
    even[0] = (zs[0][0] + zs[n // 2][0], None)
    odd[0] = (zs[0][0] - zs[n // 2][0], None)
    for k in range(1, n // 4):
        a, b = zs[k], zs[n // 2 - k]
        even[k] = (a[0] + b[0], a[1] - b[1])
        odd[k] = turned((a[0] - b[0], a[1] + b[1]), n - k, n)
    k = n // 4
    even[k] = (zs[k][0].scale(2.0), None)
    odd[k] = (zs[k][1].scale(-2.0), None)
    xe, xo = irfft(even), irfft(odd)
    out = []
    for a, b in zip(xe, xo):
        out += [a, b]
    return out


R3 = math.sqrt(0.75)


def slow_forward(load):
    parts = []
    for a in range(3):
        parts.append(rfft([V(load((16 * a + 3 * b) % SLOW)) for b in range(16)]))
    out = [None] * HALF

    def put(c, d, z):
        k = next(k for k in range(SLOW) if k % 16 == c and k % 3 == d)
        if k <= SLOW // 2:
            out[k] = z
        elif out[SLOW - k] is None:
            out[SLOW - k] = (z[0], -z[1])

    for c in range(9):
        x, y, z = parts[0][c], parts[1][c], parts[2][c]
        if x[1] is None:
            t, s = y[0] + z[0], (y[0] - z[0]).scale(R3)
            put(c, 0, (x[0] + t, None))
            put(c, 1, (x[0] - t.scale(0.5), -s))
            continue
        tr, ti = y[0] + z[0], y[1] + z[1]
        sr, si = (y[0] - z[0]).scale(R3), (y[1] - z[1]).scale(R3)
        mr, mi = x[0] - tr.scale(0.5), x[1] - ti.scale(0.5)
        put(c, 0, (x[0] + tr, x[1] + ti))
        put(c, 1, (mr + si, mi - sr))
        put(c, 2, (mr - si, mi + sr))
    return out


def slow_inverse(bins):
    def get(c, d):
        k = next(k for k in range(SLOW) if k % 16 == c and k % 3 == d)
        if k <= SLOW // 2:
            return bins[k]
        z = bins[SLOW - k]
        return (z[0], -z[1])

    mid = [[None] * 9 for _ in range(3)]
    for c in range(9):
        x, y, z = get(c, 0), get(c, 1), get(c, 2)
        if c in (0, 8):
            tr, si = y[0], y[1].scale(2.0 * R3)
            m = x[0] - tr
            mid[0][c] = (x[0] + tr.scale(2.0), None)
            mid[1][c] = (m - si, None)
            mid[2][c] = (m + si, None)
            continue
        tr, ti = y[0] + z[0], y[1] + z[1]
        sr, si = (y[0] - z[0]).scale(R3), (y[1] - z[1]).scale(R3)
        mr, mi = x[0] - tr.scale(0.5), x[1] - ti.scale(0.5)
        mid[0][c] = (x[0] + tr, x[1] + ti)
        mid[1][c] = (mr - si, mi + sr)
        mid[2][c] = (mr + si, mi - sr)
    out = [None] * SLOW
    for a in range(3):
        xs = irfft(mid[a])
        for b in range(16):
            out[(16 * a + 3 * b) % SLOW] = xs[b]
    return out


def stack2(x):
    return jnp.concatenate([x, x], axis=0)


def put(y_ref, k, re, im):
    rows = pl.ds(16 * k, 16)
    y_ref[rows, 0:128] = re
    y_ref[rows, 128:256] = im


def fast_dot(y_ref, mat_ref, out_ref):
    y = y_ref[...]
    hi = y.astype(jnp.bfloat16)
    lo = (y - hi.astype(jnp.float32)).astype(jnp.bfloat16)
    mats = jnp.concatenate([mat_ref[0:256, :], mat_ref[...]], axis=0)
    out_ref[...] = jnp.dot(jnp.concatenate([hi, lo, hi], axis=1), mats, preferred_element_type=jnp.float32)


def forward16(load, tw_ref, mat_ref, y_ref, z_ref):
    bins = slow_forward(load)
    for k in range(HALF):
        re, im = bins[k]
        if k == 0:
            xr = re.get()
            put(y_ref, 0, xr, jnp.zeros_like(xr))
            continue
        c, s = stack2(tw_ref[k, 0]), stack2(tw_ref[k, 1])
        if im is None:
            put(y_ref, k, re.get() * c, -(re.get() * s))
            continue
        cr, ci = V(re.x * c, re.neg), V(im.x * c, im.neg)
        srr, sii = V(re.x * s, re.neg), V(im.x * s, im.neg)
        put(y_ref, k, (cr + sii).get(), (ci - srr).get())
    fast_dot(y_ref, mat_ref, z_ref)


def factors(z_ref, rows=16):
    def energy(k):
        re, im = z_ref[pl.ds(16 * k, 16), 0:128], z_ref[pl.ds(16 * k, 16), 128:256]
        return re * re + im * im

    def total(ks):
        es = [energy(k) for k in ks]
        while len(es) > 1:
            es = [es[i] + es[i + 1] if i + 1 < len(es) else es[i] for i in range(0, len(es), 2)]
        return es[0]

    low, high = total(range(1, 16)), total(range(17, 24))
    e16 = energy(16)
    lane = lax.broadcasted_iota(jnp.int32, (rows, FAST), 1)
    mirror = (FAST - 1) - lane

    def flip(x):
        return jnp.concatenate([
            jnp.take_along_axis(x[0:8], mirror[0:8], axis=1, mode="promise_in_bounds"),
            jnp.take_along_axis(x[8:16], mirror[8:16], axis=1, mode="promise_in_bounds"),
        ], axis=0)

    g0 = energy(0) + low
    g1 = e16 + high + energy(24) + flip(high)
    g2 = flip(low + e16)

    def nxt(x):
        return pltpu.roll(x, FAST - 1, 1)

    def prv(x):
        return pltpu.roll(x, 1, 1)

    g01, g12 = g0 + g1, g1 + g2
    g = g01 + g2
    ga = g + nxt(g0)
    gb_next, gb_prev = g12 + nxt(g01), g01 + prv(g12)
    gc = prv(g2) + g
    g0_at1 = prv(g) + g0
    g2_at2 = g2 + nxt(g)
    phase = lane % 4
    is0, is1, is2 = phase == 0, phase == 1, phase == 2
    l0 = jnp.where(is0, ga, jnp.where(is1, g0_at1, jnp.where(is2, gb_prev, gc)))
    l1 = jnp.where(is0, ga, jnp.where(is1, gb_next, jnp.where(is2, gb_prev, gc)))
    l2 = jnp.where(is0, ga, jnp.where(is1, gb_next, jnp.where(is2, g2_at2, gc)))
    f0, f1, f2 = [lax.rsqrt(l * np.float32(1.0 / 64) + np.float32(EPS)) for l in (l0, l1, l2)]
    return f0, f1, flip(f1), flip(f2)


def weights(fs, fx):
    p0, p1, q1, q2 = [a * b for a, b in zip(fs, fx)]
    return (p0, p0 + q2, p1 + q2, p1 + q1, p1)


def group_of(k):
    return 0 if k == 0 else 1 if k < 16 else 2 if k == 16 else 3 if k < 24 else 4


def cross_inverse(load_x, load_fx, load_s, load_fs, tw_ref, mat_ref, y_ref, z_ref, store):
    hs = []
    for w in range(NWIN):
        fx = [stack2(f) for f in load_fx(w)]
        hs.append(weights(load_fs(w), fx))
    for k in range(HALF):
        cr = ci = None
        for w in range(NWIN):
            xr, xi = [stack2(x) for x in load_x(w, k)]
            sr, si = load_s(w, k)
            h = hs[w][group_of(k)]
            tr = (sr * xr + si * xi) * h
            ti = (si * xr - sr * xi) * h
            cr = tr if cr is None else cr + tr
            ci = ti if ci is None else ci + ti
        put(y_ref, k, cr, ci)
    fast_dot(y_ref, mat_ref, z_ref)
    bins = []
    for k in range(HALF):
        re, im = z_ref[pl.ds(16 * k, 16), 0:128], z_ref[pl.ds(16 * k, 16), 128:256]
        c, s = stack2(tw_ref[k, 0]), stack2(tw_ref[k, 1])
        real = re * c - im * s
        bins.append((V(real), None if k in (0, 24) else V(re * s + im * c)))
    for j, x in enumerate(slow_inverse(bins)):
        store(j, x.get())
EARLY = 8
SLOTS = 3
GROUP = 16
LINE = 8
PIECE = NFFT // GROUP
CHUNKS = ((0, 16), (16, 16), (32, 8))
MESH = pl.DeviceIdType.MESH


def gather_kernel(ids_hbm, x_ref, flat_ref, fw_hbm, tw_hbm, iv_hbm, it_hbm, xs, fx, ss, fs, iv_ref, it_ref, early,
                  ids_ref, fw_ref, tw_ref, y, z, flat, recvx, part, recv1, recv2, srcs,
                  load_sem, flat_sem, own_sem, send_x, recv_x, send1, got1, send2, got2, send3, got3):
    rec, ch = lax.axis_index("rec"), lax.axis_index("ch")
    q, x_hi = ch // 2, ch % 2
    line = x_hi * 4 + rec
    pair = rec // 2
    sibling = rec + 1 - 2 * (rec % 2)
    far = [(rec + 2) % 4, (sibling + 2) % 4]
    q_peer = [(q + i) % GROUP for i in range(1, GROUP)]
    q_id = [(rec, p * 2 + x_hi) for p in q_peer]
    l_peer = [(line + i) % LINE for i in range(1, LINE)]
    l_id = [(p % 4, q * 2 + p // 4) for p in l_peer]

    load_ids = pltpu.make_async_copy(ids_hbm, ids_ref, load_sem.at[0])
    quarter = NFFT // 4
    load_flat = [pltpu.make_async_copy(flat_ref.at[:, pl.ds(quarter * j, quarter)], flat.at[j], flat_sem.at[j]) for j in range(4)]
    load_fw = pltpu.make_async_copy(fw_hbm, fw_ref, load_sem.at[1])
    load_tw = pltpu.make_async_copy(tw_hbm, tw_ref, load_sem.at[2])
    load_own = pltpu.make_async_copy(x_ref.at[rec], recvx.at[rec], own_sem)
    load_iv = pltpu.make_async_copy(iv_hbm, iv_ref, load_sem.at[3])
    load_it = pltpu.make_async_copy(it_hbm, it_ref, load_sem.at[4])
    load_ids.start()
    for m in load_flat:
        m.start()
    barrier = pltpu.get_barrier_semaphore()
    for d in q_id + l_id:
        pl.semaphore_signal(barrier, inc=1, device_id=d, device_id_type=MESH)

    def move_x(n, peer, start, rows):
        return pltpu.make_async_remote_copy(
            src_ref=x_ref.at[peer, pl.ds(start, rows), :], dst_ref=recvx.at[rec, pl.ds(start, rows), :],
            send_sem=send_x.at[n], recv_sem=recv_x.at[n], device_id=(peer, ch), device_id_type=MESH)

    moves = []
    for c, (start, rows) in enumerate(CHUNKS):
        moves.append([move_x(2 * c + i, far[i], start, rows) for i in range(2)])
    near = move_x(6, sibling, 0, 40)

    load_ids.wait()
    row = lax.broadcasted_iota(jnp.int32, (NSRC, 160), 0)
    col = lax.broadcasted_iota(jnp.int32, (NSRC, 160), 1)
    ids = jnp.zeros((NSRC, 160), jnp.int32)
    for s in range(NSRC):
        ids = jnp.where(row == s, ids_ref[s], ids)
    here = (col // 40) * 1280 + ch * 40 + col % 40
    chooser = jnp.where(ids == here, 1.0, 0.0).astype(jnp.bfloat16)
    for j in range(GROUP):
        if j % 4 == 0:
            load_flat[j // 4].wait()
        part[j] = jnp.dot(chooser, flat[j // 4, :, pl.ds(PIECE * (j % 4), PIECE)], preferred_element_type=jnp.float32)
    recv1[q] = part[q]

    pl.semaphore_wait(barrier, GROUP - 1 + LINE - 1)

    moves[0][0].start()
    step1 = [pltpu.make_async_remote_copy(
        src_ref=part.at[p], dst_ref=recv1.at[q], send_sem=send1.at[i], recv_sem=got1.at[i],
        device_id=d, device_id_type=MESH) for i, (p, d) in enumerate(zip(q_peer, q_id))]
    for m in step1:
        m.start()
    near.start()
    for m in (load_fw, load_tw, load_own, load_iv, load_it):
        m.start()

    def keep(w, cb, half):
        for k in range(HALF):
            xs[w, cb, k] = z[pl.ds(16 * k + 8 * half, 8), :]

    def whole_block(w, p):
        rows = pl.ds(pl.multiple_of(16 * p, 16), 16)
        forward16(lambda n: recvx[w, rows, pl.ds(FAST * n, FAST)].astype(jnp.float32), tw_ref, fw_ref, y, z)
        f = factors(z)
        for half in range(2):
            keep(w, 2 * p + half, half)
            for i in range(4):
                fx[w, 2 * p + half, i] = f[i][8 * half : 8 * half + 8, :]

    def half_block(first):
        def load(n):
            return jnp.concatenate(
                [recvx[first + half, pl.ds(32, 8), pl.ds(FAST * n, FAST)].astype(jnp.float32) for half in range(2)], axis=0)

        forward16(load, tw_ref, fw_ref, y, z)
        f = factors(z)
        for half in range(2):
            keep(first + half, 4, half)
            for i in range(4):
                fx[first + half, 4, i] = f[i][8 * half : 8 * half + 8, :]

    for m in (load_fw, load_tw, load_own, load_iv, load_it):
        m.wait()

    def own(p, _):
        whole_block(rec, p)
        return 0

    lax.fori_loop(0, 2, own, 0)

    for m in step1:
        m.wait()
    total = recv1[0]
    for j in range(1, GROUP):
        total = total + recv1[j]
    recv2[line] = total
    step2 = [pltpu.make_async_remote_copy(
        src_ref=recv2.at[line], dst_ref=recv2.at[line], send_sem=send2.at[i], recv_sem=got2.at[i],
        device_id=d, device_id_type=MESH) for i, d in enumerate(l_id)]
    for m in step2 + moves[0][1:] + moves[1] + moves[2]:
        m.start()

    near.wait()

    def second(p, _):
        whole_block(sibling, p)
        return 0

    lax.fori_loop(0, 2, second, 0)

    for m in step2:
        m.wait()
    srcs[q] = jnp.concatenate([recv2[w] + recv2[4 + w] for w in range(NWIN)], axis=0).astype(jnp.bfloat16)
    step3 = [pltpu.make_async_remote_copy(
        src_ref=srcs.at[q], dst_ref=srcs.at[q], send_sem=send3.at[i], recv_sem=got3.at[i],
        device_id=d, device_id_type=MESH) for i, d in enumerate(q_id)]
    for m in step3:
        m.start()
    half_block(2 * pair)

    def far_chunk(n):
        for m in moves[n]:
            m.wait()

        def two(i, _):
            whole_block(2 * (1 - pair) + i, n)
            return 0

        lax.fori_loop(0, 2, two, 0)

    far_chunk(0)
    for m in step3:
        m.wait()

    def source_block(p, _):
        rows = pl.ds(pl.multiple_of(16 * p, 16), 16)

        def load(n):
            return srcs[n // 3, rows, pl.ds(FAST * (n % 3), FAST)].astype(jnp.float32)

        forward16(load, tw_ref, fw_ref, y, z)
        f = factors(z)
        for half in range(2):
            w = 2 * p + half
            for s in range(NSRC):
                r = 8 * half + s
                for i in range(4):
                    fs[w, s // 2, i, pl.ds(8 * (s % 2), 8), :] = jnp.broadcast_to(f[i][r : r + 1, :], (8, FAST))
                for k in range(HALF):
                    ss[w, s // 2, k, pl.ds(8 * (s % 2), 8), :] = jnp.broadcast_to(z[pl.ds(16 * k + r, 1), :], (8, 256))
        return 0

    lax.fori_loop(0, 2, source_block, 0)

    def unit(u, _):
        cb, sp = u // 4, u % 4

        def store(j, x):
            for half in range(2):
                early[2 * sp + half, pl.ds(pl.multiple_of(8 * cb, 8), 8), pl.ds(FAST * j, FAST)] = x[8 * half : 8 * half + 8]

        correlate_unit(cb, sp, xs, fx, ss, fs, it_ref, iv_ref, y, z, store)
        return 0

    lax.fori_loop(0, EARLY, unit, 0)
    far_chunk(1)
    for m in moves[2]:
        m.wait()
    half_block(2 * (1 - pair))


def correlate_unit(cb, sp, xs, fx, ss, fs, tw_ref, iv_ref, y, z, store):
    cross_inverse(
        lambda w, k: (xs[w, cb, k, :, 0:128], xs[w, cb, k, :, 128:256]),
        lambda w: [fx[w, cb, i] for i in range(4)],
        lambda w, k: (ss[w, sp, k, :, 0:128], ss[w, sp, k, :, 128:256]),
        lambda w: [fs[w, sp, i] for i in range(4)],
        tw_ref, iv_ref, y, z, store)


def correlate_kernel(xs, fx, ss, fs, iv_ref, tw_ref, early, out_ref, y, z, obuf, osem, early_sem):
    rows = 2 * EARLY
    copies = [pltpu.make_async_copy(early.at[s], out_ref.at[s, pl.ds(0, rows), :], early_sem.at[s]) for s in range(NSRC)]
    for m in copies:
        m.start()

    def send(slot, cb, sp):
        return [pltpu.make_async_copy(
            obuf.at[slot, half],
            out_ref.at[2 * sp + half, pl.ds(pl.multiple_of(8 * cb, 8), 8), :],
            osem.at[slot, half]) for half in range(2)]

    def unit(u, _):
        cb, sp = u // 4, u % 4
        slot = u % SLOTS

        @pl.when(u >= EARLY + SLOTS)
        def _():
            for m in send(slot, (u - SLOTS) // 4, (u - SLOTS) % 4):
                m.wait()

        def store(j, x):
            for half in range(2):
                obuf[slot, half, :, pl.ds(FAST * j, FAST)] = x[8 * half : 8 * half + 8]

        correlate_unit(cb, sp, xs, fx, ss, fs, tw_ref, iv_ref, y, z, store)
        for m in send(slot, cb, sp):
            m.start()
        return 0

    lax.fori_loop(EARLY, 20, unit, 0)
    for u in range(20 - SLOTS, 20):
        for m in send(u % SLOTS, u // 4, u % 4):
            m.wait()
    for m in copies:
        m.wait()


def correlate(spectra, iv, tw, early):
    channels = 8 * spectra[0].shape[1]
    vmem = pl.BlockSpec(memory_space=pltpu.VMEM)
    hbm = pl.BlockSpec(memory_space=pltpu.HBM)
    f32, dma = jnp.float32, pltpu.SemaphoreType.DMA
    return pl.pallas_call(
        correlate_kernel,
        out_shape=jax.ShapeDtypeStruct((NSRC, channels, NFFT), f32),
        in_specs=[vmem] * 7,
        out_specs=hbm,
        scratch_shapes=[
            pltpu.VMEM((ROWS, 256), f32),
            pltpu.VMEM((ROWS, 256), f32),
            pltpu.VMEM((SLOTS, 2, 8, NFFT), f32),
            dma((SLOTS, 2)),
            dma((NSRC,)),
        ],
        compiler_params=pltpu.CompilerParams(vmem_limit_bytes=32 * 2**20),
    )(*spectra, iv, tw, early)


def shards(samples, source_ids):
    fw, iv, tw = tables()
    channels = samples.shape[2]
    vmem = pl.BlockSpec(memory_space=pltpu.VMEM)
    hbm = pl.BlockSpec(memory_space=pltpu.HBM)
    f32, bf16 = jnp.float32, jnp.bfloat16
    dma = pltpu.SemaphoreType.DMA
    twist, square = pltpu.VMEM((HALF, 2, 8, FAST), f32), pltpu.VMEM((512, 256), bf16)
    spectra = pl.pallas_call(
        gather_kernel,
        out_shape=[
            jax.ShapeDtypeStruct((NWIN, 5, HALF, 8, 256), f32),
            jax.ShapeDtypeStruct((NWIN, 5, 4, 8, FAST), f32),
            jax.ShapeDtypeStruct((NWIN, 4, HALF, 16, 256), f32),
            jax.ShapeDtypeStruct((NWIN, 4, 4, 16, FAST), f32),
            jax.ShapeDtypeStruct((512, 256), bf16),
            jax.ShapeDtypeStruct((HALF, 2, 8, FAST), f32),
            jax.ShapeDtypeStruct((NSRC, 2 * EARLY, NFFT), f32),
        ],
        in_specs=[hbm] * 7,
        out_specs=[vmem] * 7,
        scratch_shapes=[
            pltpu.SMEM((NSRC,), jnp.int32),
            square,
            twist,
            pltpu.VMEM((ROWS, 256), f32),
            pltpu.VMEM((ROWS, 256), f32),
            pltpu.VMEM((4, 4 * channels, NFFT // 4), bf16),
            pltpu.VMEM((NWIN, channels, NFFT), bf16),
            pltpu.VMEM((GROUP, NSRC, PIECE), f32),
            pltpu.VMEM((GROUP, NSRC, PIECE), f32),
            pltpu.VMEM((LINE, NSRC, PIECE), f32),
            pltpu.VMEM((GROUP, NWIN * NSRC, PIECE), bf16),
            dma((5,)), dma((4,)), dma, dma((7,)), dma((7,)), dma((15,)), dma((15,)), dma((7,)), dma((7,)), dma((15,)), dma((15,)),
        ],
        compiler_params=pltpu.CompilerParams(
            collective_id=0, has_side_effects=True, vmem_limit_bytes=32 * 2**20),
    )(*[pltpu.with_memory_space_constraint(jnp.asarray(a), pltpu.HBM) for a in (
        source_ids, samples[0], samples.reshape(4 * channels, NFFT), fw, tw[:, 0:2], iv, tw[:, 2:4])])
    return correlate(spectra[0:4], *spectra[4:7])


def solution(mesh):
    return jax.shard_map(
        shards,
        mesh=mesh,
        in_specs=(P("rec", None, "ch", None), P()),
        out_specs=P(None, ("rec", "ch"), None),
        check_vma=False,
    )
```

```python
import math
import numpy as np
import jax
import jax.numpy as jnp
from jax import lax
from jax.experimental import pallas as pl
from jax.experimental.pallas import tpu as pltpu
from jax.sharding import PartitionSpec as P

NFFT = 6144
SLOW = 48
FAST = 128
HALF = 25
NSRC = 8
NWIN = 4
EPS = 1e-06
ROWS = HALF * 16


def split_bf16(a):
    hi = a.astype(jnp.bfloat16)
    lo = (np.asarray(a, np.float32) - hi.astype(np.float32)).astype(jnp.bfloat16)
    return hi, lo


def tables():
    n = np.arange(FAST)
    ang = 2.0 * np.pi * ((n[:, None] * n[None, :]) % FAST) / FAST
    c, s = np.cos(ang), np.sin(ang)
    forward = np.block([[c, -s], [s, c]]).astype(np.float32)
    inverse = np.block([[c, s], [-s, c]]).astype(np.float32)
    fhi, flo = split_bf16(forward)
    ihi, ilo = split_bf16(inverse)
    fw = np.concatenate([fhi, flo], axis=0)
    iv = np.concatenate([ihi, ilo], axis=0)
    k1 = np.arange(HALF)[:, None]
    turn = 2.0 * np.pi * (k1 * n[None, :]) / NFFT
    scale = ((-1.0) ** k1) / math.sqrt(NWIN * NFFT)
    tw = np.stack([np.cos(turn), np.sin(turn), np.cos(turn) * scale, np.sin(turn) * scale], axis=1)
    tw = np.broadcast_to(tw[:, :, None, :], (HALF, 4, 8, FAST)).astype(np.float32)
    return fw, iv, np.ascontiguousarray(tw)


class V:
    def __init__(self, x, neg=False):
        self.x, self.neg = x, neg

    def __neg__(self):
        return V(self.x, not self.neg)

    def __add__(self, o):
        if self.neg == o.neg:
            return V(self.x + o.x, self.neg)
        return V(o.x - self.x) if self.neg else V(self.x - o.x)

    def __sub__(self, o):
        return self + (-o)

    def scale(self, f):
        if abs(f - 1.0) < 1e-12:
            return self
        return V(self.x * np.float32(abs(f)), self.neg != (f < 0))

    def get(self):
        return -self.x if self.neg else self.x


def turned(z, quarter, size):
    re, im = z
    step = (quarter * (16 // size)) % 16
    if step == 0:
        return z
    if step == 4:
        return im, -re
    if step == 12:
        return -im, re
    if step == 8:
        return -re, -im
    root = math.sqrt(0.5)
    if step == 2:
        return (re + im).scale(root), (im - re).scale(root)
    if step == 14:
        return (re - im).scale(root), (im + re).scale(root)
    c, s = math.cos(2 * math.pi * step / 16), math.sin(2 * math.pi * step / 16)
    return re.scale(c) + im.scale(s), im.scale(c) - re.scale(s)


def rfft(xs):
    n = len(xs)
    if n == 2:
        return [(xs[0] + xs[1], None), (xs[0] - xs[1], None)]
    even, odd = rfft(xs[0::2]), rfft(xs[1::2])
    out = [None] * (n // 2 + 1)
    out[0] = (even[0][0] + odd[0][0], None)
    out[n // 2] = (even[0][0] - odd[0][0], None)
    for k in range(1, n // 4):
        t = turned(odd[k], k, n)
        e = even[k]
        out[k] = (e[0] + t[0], e[1] + t[1])
        out[n // 2 - k] = (e[0] - t[0], t[1] - e[1])
    if n >= 4:
        k = n // 4
        out[k] = (even[k][0], -odd[k][0])
    return out


def irfft(zs):
    n = 2 * (len(zs) - 1)
    if n == 2:
        return [zs[0][0] + zs[1][0], zs[0][0] - zs[1][0]]
    even, odd = [None] * (n // 4 + 1), [None] * (n // 4 + 1)
    even[0] = (zs[0][0] + zs[n // 2][0], None)
    odd[0] = (zs[0][0] - zs[n // 2][0], None)
    for k in range(1, n // 4):
        a, b = zs[k], zs[n // 2 - k]
        even[k] = (a[0] + b[0], a[1] - b[1])
        odd[k] = turned((a[0] - b[0], a[1] + b[1]), n - k, n)
    k = n // 4
    even[k] = (zs[k][0], None)
    odd[k] = (-zs[k][1], None)
    xe, xo = irfft(even), irfft(odd)
    out = []
    for a, b in zip(xe, xo):
        out += [a, b]
    return out


R3 = math.sqrt(0.75)


def slow_forward(load):
    parts = []
    for a in range(3):
        parts.append(rfft([V(load((16 * a + 3 * b) % SLOW)) for b in range(16)]))
    out = [None] * HALF

    def put(c, d, z):
        k = next(k for k in range(SLOW) if k % 16 == c and k % 3 == d)
        if k <= SLOW // 2:
            out[k] = z
        elif out[SLOW - k] is None:
            out[SLOW - k] = (z[0], -z[1])

    for c in range(9):
        x, y, z = parts[0][c], parts[1][c], parts[2][c]
        if x[1] is None:
            t, s = y[0] + z[0], (y[0] - z[0]).scale(R3)
            put(c, 0, (x[0] + t, None))
            put(c, 1, (x[0] - t.scale(0.5), -s))
            continue
        tr, ti = y[0] + z[0], y[1] + z[1]
        sr, si = (y[0] - z[0]).scale(R3), (y[1] - z[1]).scale(R3)
        mr, mi = x[0] - tr.scale(0.5), x[1] - ti.scale(0.5)
        put(c, 0, (x[0] + tr, x[1] + ti))
        put(c, 1, (mr + si, mi - sr))
        put(c, 2, (mr - si, mi + sr))
    return out


def slow_inverse(bins):
    def get(c, d):
        k = next(k for k in range(SLOW) if k % 16 == c and k % 3 == d)
        if k <= SLOW // 2:
            return bins[k]
        z = bins[SLOW - k]
        return (z[0], -z[1])

    mid = [[None] * 9 for _ in range(3)]
    for c in range(9):
        x, y, z = get(c, 0), get(c, 1), get(c, 2)
        if c in (0, 8):
            tr, si = y[0], y[1].scale(R3)
            m = x[0] - tr.scale(0.5)
            mid[0][c] = (x[0] + tr, None)
            mid[1][c] = (m - si, None)
            mid[2][c] = (m + si, None)
            continue
        tr, ti = y[0] + z[0], y[1] + z[1]
        sr, si = (y[0] - z[0]).scale(R3), (y[1] - z[1]).scale(R3)
        mr, mi = x[0] - tr.scale(0.5), x[1] - ti.scale(0.5)
        mid[0][c] = (x[0] + tr, x[1] + ti)
        mid[1][c] = (mr - si, mi + sr)
        mid[2][c] = (mr + si, mi - sr)
    out = [None] * SLOW
    for a in range(3):
        xs = irfft(mid[a])
        for b in range(16):
            out[(16 * a + 3 * b) % SLOW] = xs[b]
    return out


def stack2(x):
    return jnp.concatenate([x, x], axis=0)


def put(y_ref, k, re, im):
    rows = pl.ds(16 * k, 16)
    y_ref[rows, 0:128] = re
    y_ref[rows, 128:256] = im


def fast_dot(y_ref, mat_ref, out_ref):
    y = y_ref[...]
    hi = y.astype(jnp.bfloat16)
    lo = (y - hi.astype(jnp.float32)).astype(jnp.bfloat16)
    mats = jnp.concatenate([mat_ref[0:256, :], mat_ref[...]], axis=0)
    out_ref[...] = jnp.dot(jnp.concatenate([hi, lo, hi], axis=1), mats, preferred_element_type=jnp.float32)


def forward16(load, tw_ref, mat_ref, y_ref, z_ref):
    bins = slow_forward(load)
    for k in range(HALF):
        re, im = bins[k]
        if k == 0:
            xr = re.get()
            put(y_ref, 0, xr, jnp.zeros_like(xr))
            continue
        c, s = stack2(tw_ref[k, 0]), stack2(tw_ref[k, 1])
        if im is None:
            put(y_ref, k, re.get() * c, -(re.get() * s))
            continue
        cr, ci = V(re.x * c, re.neg), V(im.x * c, im.neg)
        srr, sii = V(re.x * s, re.neg), V(im.x * s, im.neg)
        put(y_ref, k, (cr + sii).get(), (ci - srr).get())
    fast_dot(y_ref, mat_ref, z_ref)


def factors(z_ref, rows=16):
    def energy(k):
        re, im = z_ref[pl.ds(16 * k, 16), 0:128], z_ref[pl.ds(16 * k, 16), 128:256]
        return re * re + im * im

    def total(ks):
        es = [energy(k) for k in ks]
        while len(es) > 1:
            es = [es[i] + es[i + 1] if i + 1 < len(es) else es[i] for i in range(0, len(es), 2)]
        return es[0]

    low, high = total(range(1, 16)), total(range(17, 24))
    e16 = energy(16)
    lane = lax.broadcasted_iota(jnp.int32, (rows, FAST), 1)
    mirror = (FAST - 1) - lane

    def flip(x):
        return jnp.concatenate([
            jnp.take_along_axis(x[0:8], mirror[0:8], axis=1, mode="promise_in_bounds"),
            jnp.take_along_axis(x[8:16], mirror[8:16], axis=1, mode="promise_in_bounds"),
        ], axis=0)

    g0 = energy(0) + low
    g1 = e16 + high + energy(24) + flip(high)
    g2 = flip(low + e16)

    def nxt(x):
        return pltpu.roll(x, FAST - 1, 1)

    def prv(x):
        return pltpu.roll(x, 1, 1)

    g01, g12 = g0 + g1, g1 + g2
    g = g01 + g2
    ga = g + nxt(g0)
    gb_next, gb_prev = g12 + nxt(g01), g01 + prv(g12)
    gc = prv(g2) + g
    g0_at1 = prv(g) + g0
    g2_at2 = g2 + nxt(g)
    phase = lane % 4
    is0, is1, is2 = phase == 0, phase == 1, phase == 2
    l0 = jnp.where(is0, ga, jnp.where(is1, g0_at1, jnp.where(is2, gb_prev, gc)))
    l1 = jnp.where(is0, ga, jnp.where(is1, gb_next, jnp.where(is2, gb_prev, gc)))
    l2 = jnp.where(is0, ga, jnp.where(is1, gb_next, jnp.where(is2, g2_at2, gc)))
    f0, f1, f2 = [lax.rsqrt(l * np.float32(1.0 / 64) + np.float32(EPS)) for l in (l0, l1, l2)]
    return f0, f1, flip(f1), flip(f2)


def weights(fs, fx):
    p0, p1, q1, q2 = [a * b for a, b in zip(fs, fx)]
    return (p0, p0 + q2, p1 + q2, p1 + q1, p1)


def group_of(k):
    return 0 if k == 0 else 1 if k < 16 else 2 if k == 16 else 3 if k < 24 else 4


def cross_inverse(load_x, load_fx, load_s, load_fs, tw_ref, mat_ref, y_ref, z_ref, store):
    hs = []
    for w in range(NWIN):
        fx = [stack2(f) for f in load_fx(w)]
        hs.append(weights(load_fs(w), fx))
    for k in range(HALF):
        cr = ci = None
        for w in range(NWIN):
            xr, xi = [stack2(x) for x in load_x(w, k)]
            sr, si = load_s(w, k)
            h = hs[w][group_of(k)]
            tr = (sr * xr + si * xi) * h
            ti = (si * xr - sr * xi) * h
            cr = tr if cr is None else cr + tr
            ci = ti if ci is None else ci + ti
        put(y_ref, k, cr, ci)
    fast_dot(y_ref, mat_ref, z_ref)
    bins = []
    for k in range(HALF):
        re, im = z_ref[pl.ds(16 * k, 16), 0:128], z_ref[pl.ds(16 * k, 16), 128:256]
        c, s = stack2(tw_ref[k, 0]), stack2(tw_ref[k, 1])
        real = re * c - im * s
        bins.append((V(real), None if k in (0, 24) else V(re * s + im * c)))
    for j, x in enumerate(slow_inverse(bins)):
        store(j, x.get())
EARLY = 8
SLOTS = 3
GROUP = 16
LINE = 8
PIECE = NFFT // GROUP
CHUNKS = ((0, 16), (16, 16), (32, 8))
MESH = pl.DeviceIdType.MESH


def gather_kernel(ids_hbm, x_ref, flat_ref, fw_hbm, tw_hbm, iv_hbm, it_hbm, xs, fx, ss, fs, iv_ref, it_ref, early,
                  ids_ref, fw_ref, tw_ref, y, z, flat, recvx, part, recv1, recv2, srcs,
                  load_sem, flat_sem, own_sem, send_x, recv_x, send1, got1, send2, got2, send3, got3):
    rec, ch = lax.axis_index("rec"), lax.axis_index("ch")
    q, x_hi = ch // 2, ch % 2
    line = x_hi * 4 + rec
    pair, core = rec // 2, rec % 2
    sibling = rec + 1 - 2 * (rec % 2)
    far = [(rec + 2) % 4, (sibling + 2) % 4]
    hops = lambda offset: sum(min(d, 4 - d) for d in offset)
    offsets = sorted(((a, b) for a in range(4) for b in range(4) if a or b), key=hops, reverse=True)
    q_peer = [(q // 4 + a) % 4 * 4 + (q % 4 + b) % 4 for a, b in offsets]
    q_id = [(rec, p * 2 + x_hi) for p in q_peer]
    l_peer = [(line // 2 + i) % 4 * 2 + (line + j) % 2 for i, j in ((2, 0), (2, 1), (1, 0), (3, 0), (1, 1), (3, 1), (0, 1))]
    l_id = [(p % 4, q * 2 + p // 4) for p in l_peer]

    load_ids = pltpu.make_async_copy(ids_hbm, ids_ref, load_sem.at[0])
    quarter = NFFT // 4
    load_flat = [pltpu.make_async_copy(flat_ref.at[:, pl.ds(quarter * j, quarter)], flat.at[j], flat_sem.at[j]) for j in range(4)]
    load_fw = pltpu.make_async_copy(fw_hbm, fw_ref, load_sem.at[1])
    load_tw = pltpu.make_async_copy(tw_hbm, tw_ref, load_sem.at[2])
    load_own = pltpu.make_async_copy(x_ref.at[rec], recvx.at[rec], own_sem)
    load_iv = pltpu.make_async_copy(iv_hbm, iv_ref, load_sem.at[3])
    load_it = pltpu.make_async_copy(it_hbm, it_ref, load_sem.at[4])
    load_ids.start()
    for m in load_flat:
        m.start()
    barrier = pltpu.get_barrier_semaphore()
    for d in q_id + l_id:
        pl.semaphore_signal(barrier, inc=1, device_id=d, device_id_type=MESH)

    def move_x(n, peer, start, rows):
        return pltpu.make_async_remote_copy(
            src_ref=x_ref.at[peer, pl.ds(start, rows), :], dst_ref=recvx.at[rec, pl.ds(start, rows), :],
            send_sem=send_x.at[n], recv_sem=recv_x.at[n], device_id=(peer, ch), device_id_type=MESH)

    moves = []
    for c, (start, rows) in enumerate(CHUNKS):
        moves.append([move_x(2 * c + i, far[i], start, rows) for i in range(2)])
    near = move_x(6, sibling, 0, 40)

    load_ids.wait()
    row = lax.broadcasted_iota(jnp.int32, (NSRC, 160), 0)
    col = lax.broadcasted_iota(jnp.int32, (NSRC, 160), 1)
    ids = jnp.zeros((NSRC, 160), jnp.int32)
    for s in range(NSRC):
        ids = jnp.where(row == s, ids_ref[s], ids)
    here = (col // 40) * 1280 + ch * 40 + col % 40
    chooser = jnp.where(ids == here, 1.0, 0.0).astype(jnp.bfloat16)
    for j in range(GROUP):
        if j % 4 == 0:
            load_flat[j // 4].wait()
        part[j] = jnp.dot(chooser, flat[j // 4, :, pl.ds(PIECE * (j % 4), PIECE)], preferred_element_type=jnp.float32)
    recv1[q] = part[q]

    pl.semaphore_wait(barrier, GROUP - 1 + LINE - 1)
    moves[0][0].start()
    step1 = [pltpu.make_async_remote_copy(
        src_ref=part.at[p], dst_ref=recv1.at[q], send_sem=send1.at[i], recv_sem=got1.at[i],
        device_id=d, device_id_type=MESH) for i, (p, d) in enumerate(zip(q_peer, q_id))]
    for m in step1:
        m.start()
    near.start()
    for m in (load_fw, load_tw, load_own, load_iv, load_it):
        m.start()

    def keep(w, cb, half):
        for k in range(HALF):
            xs[w, cb, k] = z[pl.ds(16 * k + 8 * half, 8), :]

    def whole_block(w, p):
        rows = pl.ds(pl.multiple_of(16 * p, 16), 16)
        forward16(lambda n: recvx[w, rows, pl.ds(FAST * n, FAST)].astype(jnp.float32), tw_ref, fw_ref, y, z)
        f = factors(z)
        for half in range(2):
            keep(w, 2 * p + half, half)
            for i in range(4):
                fx[w, 2 * p + half, i] = f[i][8 * half : 8 * half + 8, :]

    def half_block(first):
        def load(n):
            return jnp.concatenate(
                [recvx[first + half, pl.ds(32, 8), pl.ds(FAST * n, FAST)].astype(jnp.float32) for half in range(2)], axis=0)

        forward16(load, tw_ref, fw_ref, y, z)
        f = factors(z)
        for half in range(2):
            keep(first + half, 4, half)
            for i in range(4):
                fx[first + half, 4, i] = f[i][8 * half : 8 * half + 8, :]

    for m in (load_fw, load_tw, load_own, load_iv, load_it):
        m.wait()

    def own(p, _):
        whole_block(rec, p)
        return 0

    lax.fori_loop(0, 2, own, 0)

    for m in step1:
        m.wait_recv()
    total = recv1[0]
    for j in range(1, GROUP):
        total = total + recv1[j]
    recv2[line] = total
    step2 = [pltpu.make_async_remote_copy(
        src_ref=recv2.at[line], dst_ref=recv2.at[line], send_sem=send2.at[i], recv_sem=got2.at[i],
        device_id=d, device_id_type=MESH) for i, d in enumerate(l_id)]
    for m in step2 + moves[0][1:] + moves[1] + moves[2]:
        m.start()

    near.wait_recv()

    def second(p, _):
        whole_block(sibling, p)
        return 0

    lax.fori_loop(0, 2, second, 0)

    for m in step2:
        m.wait_recv()
    srcs[core, q] = jnp.concatenate(
        [recv2[2 * core + i] + recv2[4 + 2 * core + i] for i in range(2)], axis=0).astype(jnp.bfloat16)
    step3 = [pltpu.make_async_remote_copy(
        src_ref=srcs.at[core, q], dst_ref=srcs.at[core, q], send_sem=send3.at[i], recv_sem=got3.at[i],
        device_id=d, device_id_type=MESH) for i, d in enumerate(q_id)]
    for m in step3:
        m.start()
    half_block(2 * pair)

    def far_chunk(n):
        for m in moves[n]:
            m.wait_recv()

        def two(i, _):
            whole_block(2 * (1 - pair) + i, n)
            return 0

        lax.fori_loop(0, 2, two, 0)

    far_chunk(0)
    for m in step3:
        m.wait_recv()

    share = pltpu.make_async_remote_copy(
        src_ref=srcs.at[core], dst_ref=srcs.at[core], send_sem=send_x.at[7], recv_sem=recv_x.at[7],
        device_id=(sibling, ch), device_id_type=MESH)
    share.start()

    def source_block(i, _):
        p = (core + i) % 2

        @pl.when(i == 1)
        def _():
            share.wait_recv()

        def load(n):
            return srcs[p, n // 3, :, pl.ds(FAST * (n % 3), FAST)].astype(jnp.float32)

        forward16(load, tw_ref, fw_ref, y, z)
        f = factors(z)
        for half in range(2):
            w = 2 * p + half
            for s in range(NSRC):
                r = 8 * half + s
                for i in range(4):
                    fs[w, s // 2, i, pl.ds(8 * (s % 2), 8), :] = jnp.broadcast_to(f[i][r : r + 1, :], (8, FAST))
                for k in range(HALF):
                    ss[w, s // 2, k, pl.ds(8 * (s % 2), 8), :] = jnp.broadcast_to(z[pl.ds(16 * k + r, 1), :], (8, 256))
        return 0

    lax.fori_loop(0, 2, source_block, 0)

    def unit(u, _):
        cb, sp = u // 4, u % 4

        def store(j, x):
            for half in range(2):
                early[2 * sp + half, pl.ds(pl.multiple_of(8 * cb, 8), 8), pl.ds(FAST * j, FAST)] = x[8 * half : 8 * half + 8]

        correlate_unit(cb, sp, xs, fx, ss, fs, it_ref, iv_ref, y, z, store)
        return 0

    lax.fori_loop(0, EARLY, unit, 0)
    far_chunk(1)
    for m in moves[2]:
        m.wait_recv()
    half_block(2 * (1 - pair))
    for m in step1 + step2 + step3 + moves[0] + moves[1] + moves[2] + [near, share]:
        m.wait_send()


def correlate_unit(cb, sp, xs, fx, ss, fs, tw_ref, iv_ref, y, z, store):
    cross_inverse(
        lambda w, k: (xs[w, cb, k, :, 0:128], xs[w, cb, k, :, 128:256]),
        lambda w: [fx[w, cb, i] for i in range(4)],
        lambda w, k: (ss[w, sp, k, :, 0:128], ss[w, sp, k, :, 128:256]),
        lambda w: [fs[w, sp, i] for i in range(4)],
        tw_ref, iv_ref, y, z, store)


def correlate_kernel(xs, fx, ss, fs, iv_ref, tw_ref, early, out_ref, y, z, obuf, osem, early_sem):
    rows = 2 * EARLY
    copies = [pltpu.make_async_copy(early.at[s], out_ref.at[s, pl.ds(0, rows), :], early_sem.at[s]) for s in range(NSRC)]
    for m in copies:
        m.start()

    def send(slot, cb, sp):
        return [pltpu.make_async_copy(
            obuf.at[slot, half],
            out_ref.at[2 * sp + half, pl.ds(pl.multiple_of(8 * cb, 8), 8), :],
            osem.at[slot, half]) for half in range(2)]

    def unit(u, _):
        cb, sp = u // 4, u % 4
        slot = u % SLOTS

        @pl.when(u >= EARLY + SLOTS)
        def _():
            for m in send(slot, (u - SLOTS) // 4, (u - SLOTS) % 4):
                m.wait()

        def store(j, x):
            for half in range(2):
                obuf[slot, half, :, pl.ds(FAST * j, FAST)] = x[8 * half : 8 * half + 8]

        correlate_unit(cb, sp, xs, fx, ss, fs, tw_ref, iv_ref, y, z, store)
        for m in send(slot, cb, sp):
            m.start()
        return 0

    lax.fori_loop(EARLY, 20, unit, 0)
    for u in range(20 - SLOTS, 20):
        for m in send(u % SLOTS, u // 4, u % 4):
            m.wait()
    for m in copies:
        m.wait()


def correlate(spectra, iv, tw, early):
    channels = 8 * spectra[0].shape[1]
    vmem = pl.BlockSpec(memory_space=pltpu.VMEM)
    hbm = pl.BlockSpec(memory_space=pltpu.HBM)
    f32, dma = jnp.float32, pltpu.SemaphoreType.DMA
    return pl.pallas_call(
        correlate_kernel,
        out_shape=jax.ShapeDtypeStruct((NSRC, channels, NFFT), f32),
        in_specs=[vmem] * 7,
        out_specs=hbm,
        scratch_shapes=[
            pltpu.VMEM((ROWS, 256), f32),
            pltpu.VMEM((ROWS, 256), f32),
            pltpu.VMEM((SLOTS, 2, 8, NFFT), f32),
            dma((SLOTS, 2)),
            dma((NSRC,)),
        ],
        compiler_params=pltpu.CompilerParams(vmem_limit_bytes=32 * 2**20),
    )(*spectra, iv, tw, early)


def shards(samples, source_ids):
    fw, iv, tw = tables()
    channels = samples.shape[2]
    vmem = pl.BlockSpec(memory_space=pltpu.VMEM)
    hbm = pl.BlockSpec(memory_space=pltpu.HBM)
    f32, bf16 = jnp.float32, jnp.bfloat16
    dma = pltpu.SemaphoreType.DMA
    twist, square = pltpu.VMEM((HALF, 2, 8, FAST), f32), pltpu.VMEM((512, 256), bf16)
    spectra = pl.pallas_call(
        gather_kernel,
        out_shape=[
            jax.ShapeDtypeStruct((NWIN, 5, HALF, 8, 256), f32),
            jax.ShapeDtypeStruct((NWIN, 5, 4, 8, FAST), f32),
            jax.ShapeDtypeStruct((NWIN, 4, HALF, 16, 256), f32),
            jax.ShapeDtypeStruct((NWIN, 4, 4, 16, FAST), f32),
            jax.ShapeDtypeStruct((512, 256), bf16),
            jax.ShapeDtypeStruct((HALF, 2, 8, FAST), f32),
            jax.ShapeDtypeStruct((NSRC, 2 * EARLY, NFFT), f32),
        ],
        in_specs=[hbm] * 7,
        out_specs=[vmem] * 7,
        scratch_shapes=[
            pltpu.SMEM((NSRC,), jnp.int32),
            square,
            twist,
            pltpu.VMEM((ROWS, 256), f32),
            pltpu.VMEM((ROWS, 256), f32),
            pltpu.VMEM((4, 4 * channels, NFFT // 4), bf16),
            pltpu.VMEM((NWIN, channels, NFFT), bf16),
            pltpu.VMEM((GROUP, NSRC, PIECE), f32),
            pltpu.VMEM((GROUP, NSRC, PIECE), f32),
            pltpu.VMEM((LINE, NSRC, PIECE), f32),
            pltpu.VMEM((2, GROUP, 2 * NSRC, PIECE), bf16),
            dma((5,)), dma((4,)), dma, dma((8,)), dma((8,)), dma((15,)), dma((15,)), dma((7,)), dma((7,)), dma((15,)), dma((15,)),
        ],
        compiler_params=pltpu.CompilerParams(
            collective_id=0, has_side_effects=True, vmem_limit_bytes=32 * 2**20),
    )(*[pltpu.with_memory_space_constraint(jnp.asarray(a), pltpu.HBM) for a in (
        source_ids, samples[0], samples.reshape(4 * channels, NFFT), fw, tw[:, 0:2], iv, tw[:, 2:4])])
    return correlate(spectra[0:4], *spectra[4:7])


def solution(mesh):
    return jax.shard_map(
        shards,
        mesh=mesh,
        in_specs=(P("rec", None, "ch", None), P()),
        out_specs=P(None, ("rec", "ch"), None),
        check_vma=False,
    )
```

```python
import math
import numpy as np
import jax
import jax.numpy as jnp
from jax import lax
from jax.experimental import pallas as pl
from jax.experimental.pallas import tpu as pltpu
from jax.sharding import PartitionSpec as P

NFFT = 6144
SLOW = 48
FAST = 128
HALF = 25
NSRC = 8
NWIN = 4
EPS = 1e-06
ROWS = HALF * 16


def split_bf16(a):
    hi = a.astype(jnp.bfloat16)
    lo = (np.asarray(a, np.float32) - hi.astype(np.float32)).astype(jnp.bfloat16)
    return hi, lo


def tables():
    n = np.arange(FAST)
    ang = 2.0 * np.pi * ((n[:, None] * n[None, :]) % FAST) / FAST
    c, s = np.cos(ang), np.sin(ang)
    forward = np.block([[c, -s], [s, c]]).astype(np.float32)
    inverse = np.block([[c, s], [-s, c]]).astype(np.float32)
    fhi, flo = split_bf16(forward)
    ihi, ilo = split_bf16(inverse)
    fw = np.concatenate([fhi, flo], axis=0)
    iv = np.concatenate([ihi, ilo], axis=0)
    k1 = np.arange(HALF)[:, None]
    turn = 2.0 * np.pi * (k1 * n[None, :]) / NFFT
    scale = ((-1.0) ** k1) / math.sqrt(NWIN * NFFT)
    tw = np.stack([np.cos(turn), np.sin(turn), np.cos(turn) * scale, np.sin(turn) * scale], axis=1)
    tw = np.broadcast_to(tw[:, :, None, :], (HALF, 4, 8, FAST)).astype(np.float32)
    return fw, iv, np.ascontiguousarray(tw)


class V:
    def __init__(self, x, neg=False):
        self.x, self.neg = x, neg

    def __neg__(self):
        return V(self.x, not self.neg)

    def __add__(self, o):
        if self.neg == o.neg:
            return V(self.x + o.x, self.neg)
        return V(o.x - self.x) if self.neg else V(self.x - o.x)

    def __sub__(self, o):
        return self + (-o)

    def scale(self, f):
        if abs(f - 1.0) < 1e-12:
            return self
        return V(self.x * np.float32(abs(f)), self.neg != (f < 0))

    def get(self):
        return -self.x if self.neg else self.x


def turned(z, quarter, size):
    re, im = z
    step = (quarter * (16 // size)) % 16
    if step == 0:
        return z
    if step == 4:
        return im, -re
    if step == 12:
        return -im, re
    if step == 8:
        return -re, -im
    root = math.sqrt(0.5)
    if step == 2:
        return (re + im).scale(root), (im - re).scale(root)
    if step == 14:
        return (re - im).scale(root), (im + re).scale(root)
    c, s = math.cos(2 * math.pi * step / 16), math.sin(2 * math.pi * step / 16)
    return re.scale(c) + im.scale(s), im.scale(c) - re.scale(s)


def rfft(xs):
    n = len(xs)
    if n == 2:
        return [(xs[0] + xs[1], None), (xs[0] - xs[1], None)]
    even, odd = rfft(xs[0::2]), rfft(xs[1::2])
    out = [None] * (n // 2 + 1)
    out[0] = (even[0][0] + odd[0][0], None)
    out[n // 2] = (even[0][0] - odd[0][0], None)
    for k in range(1, n // 4):
        t = turned(odd[k], k, n)
        e = even[k]
        out[k] = (e[0] + t[0], e[1] + t[1])
        out[n // 2 - k] = (e[0] - t[0], t[1] - e[1])
    if n >= 4:
        k = n // 4
        out[k] = (even[k][0], -odd[k][0])
    return out


def irfft(zs):
    n = 2 * (len(zs) - 1)
    if n == 2:
        return [zs[0][0] + zs[1][0], zs[0][0] - zs[1][0]]
    even, odd = [None] * (n // 4 + 1), [None] * (n // 4 + 1)
    even[0] = (zs[0][0] + zs[n // 2][0], None)
    odd[0] = (zs[0][0] - zs[n // 2][0], None)
    for k in range(1, n // 4):
        a, b = zs[k], zs[n // 2 - k]
        even[k] = (a[0] + b[0], a[1] - b[1])
        odd[k] = turned((a[0] - b[0], a[1] + b[1]), n - k, n)
    k = n // 4
    even[k] = (zs[k][0], None)
    odd[k] = (-zs[k][1], None)
    xe, xo = irfft(even), irfft(odd)
    out = []
    for a, b in zip(xe, xo):
        out += [a, b]
    return out


R3 = math.sqrt(0.75)


def slow_forward(load):
    parts = []
    for a in range(3):
        parts.append(rfft([V(load((16 * a + 3 * b) % SLOW)) for b in range(16)]))
    out = [None] * HALF

    def put(c, d, z):
        k = next(k for k in range(SLOW) if k % 16 == c and k % 3 == d)
        if k <= SLOW // 2:
            out[k] = z
        elif out[SLOW - k] is None:
            out[SLOW - k] = (z[0], -z[1])

    for c in range(9):
        x, y, z = parts[0][c], parts[1][c], parts[2][c]
        if x[1] is None:
            t, s = y[0] + z[0], (y[0] - z[0]).scale(R3)
            put(c, 0, (x[0] + t, None))
            put(c, 1, (x[0] - t.scale(0.5), -s))
            continue
        tr, ti = y[0] + z[0], y[1] + z[1]
        sr, si = (y[0] - z[0]).scale(R3), (y[1] - z[1]).scale(R3)
        mr, mi = x[0] - tr.scale(0.5), x[1] - ti.scale(0.5)
        put(c, 0, (x[0] + tr, x[1] + ti))
        put(c, 1, (mr + si, mi - sr))
        put(c, 2, (mr - si, mi + sr))
    return out


def slow_inverse(bins):
    def get(c, d):
        k = next(k for k in range(SLOW) if k % 16 == c and k % 3 == d)
        if k <= SLOW // 2:
            return bins[k]
        z = bins[SLOW - k]
        return (z[0], -z[1])

    mid = [[None] * 9 for _ in range(3)]
    for c in range(9):
        x, y, z = get(c, 0), get(c, 1), get(c, 2)
        if c in (0, 8):
            tr, si = y[0], y[1].scale(R3)
            m = x[0] - tr.scale(0.5)
            mid[0][c] = (x[0] + tr, None)
            mid[1][c] = (m - si, None)
            mid[2][c] = (m + si, None)
            continue
        tr, ti = y[0] + z[0], y[1] + z[1]
        sr, si = (y[0] - z[0]).scale(R3), (y[1] - z[1]).scale(R3)
        mr, mi = x[0] - tr.scale(0.5), x[1] - ti.scale(0.5)
        mid[0][c] = (x[0] + tr, x[1] + ti)
        mid[1][c] = (mr - si, mi + sr)
        mid[2][c] = (mr + si, mi - sr)
    out = [None] * SLOW
    for a in range(3):
        xs = irfft(mid[a])
        for b in range(16):
            out[(16 * a + 3 * b) % SLOW] = xs[b]
    return out


def stack2(x):
    return jnp.concatenate([x, x], axis=0)


def put(y_ref, k, re, im):
    rows = pl.ds(16 * k, 16)
    y_ref[rows, 0:128] = re
    y_ref[rows, 128:256] = im


def fast_dot(y_ref, mat_ref, out_ref):
    y = y_ref[...]
    hi = y.astype(jnp.bfloat16)
    lo = (y - hi.astype(jnp.float32)).astype(jnp.bfloat16)
    mats = jnp.concatenate([mat_ref[0:256, :], mat_ref[...]], axis=0)
    out_ref[...] = jnp.dot(jnp.concatenate([hi, lo, hi], axis=1), mats, preferred_element_type=jnp.float32)


def forward16(load, tw_ref, mat_ref, y_ref, z_ref):
    bins = slow_forward(load)
    for k in range(HALF):
        re, im = bins[k]
        if k == 0:
            xr = re.get()
            put(y_ref, 0, xr, jnp.zeros_like(xr))
            continue
        c, s = stack2(tw_ref[k, 0]), stack2(tw_ref[k, 1])
        if im is None:
            put(y_ref, k, re.get() * c, -(re.get() * s))
            continue
        cr, ci = V(re.x * c, re.neg), V(im.x * c, im.neg)
        srr, sii = V(re.x * s, re.neg), V(im.x * s, im.neg)
        put(y_ref, k, (cr + sii).get(), (ci - srr).get())
    fast_dot(y_ref, mat_ref, z_ref)


def factors(z_ref, rows=16):
    def energy(k):
        re, im = z_ref[pl.ds(16 * k, 16), 0:128], z_ref[pl.ds(16 * k, 16), 128:256]
        return re * re + im * im

    def total(ks):
        es = [energy(k) for k in ks]
        while len(es) > 1:
            es = [es[i] + es[i + 1] if i + 1 < len(es) else es[i] for i in range(0, len(es), 2)]
        return es[0]

    low, high = total(range(1, 16)), total(range(17, 24))
    e16 = energy(16)
    lane = lax.broadcasted_iota(jnp.int32, (rows, FAST), 1)
    mirror = (FAST - 1) - lane

    def flip(x):
        return jnp.concatenate([
            jnp.take_along_axis(x[0:8], mirror[0:8], axis=1, mode="promise_in_bounds"),
            jnp.take_along_axis(x[8:16], mirror[8:16], axis=1, mode="promise_in_bounds"),
        ], axis=0)

    g0 = energy(0) + low
    g1 = e16 + high + energy(24) + flip(high)
    g2 = flip(low + e16)

    def nxt(x):
        return pltpu.roll(x, FAST - 1, 1)

    def prv(x):
        return pltpu.roll(x, 1, 1)

    g01, g12 = g0 + g1, g1 + g2
    g = g01 + g2
    ga = g + nxt(g0)
    gb_next, gb_prev = g12 + nxt(g01), g01 + prv(g12)
    gc = prv(g2) + g
    g0_at1 = prv(g) + g0
    g2_at2 = g2 + nxt(g)
    phase = lane % 4
    is0, is1, is2 = phase == 0, phase == 1, phase == 2
    l0 = jnp.where(is0, ga, jnp.where(is1, g0_at1, jnp.where(is2, gb_prev, gc)))
    l1 = jnp.where(is0, ga, jnp.where(is1, gb_next, jnp.where(is2, gb_prev, gc)))
    l2 = jnp.where(is0, ga, jnp.where(is1, gb_next, jnp.where(is2, g2_at2, gc)))
    f0, f1, f2 = [lax.rsqrt(l * np.float32(1.0 / 64) + np.float32(EPS)) for l in (l0, l1, l2)]
    return f0, f1, flip(f1), flip(f2)


def weights(fs, fx):
    p0, p1, q1, q2 = [a * b for a, b in zip(fs, fx)]
    return (p0, p0 + q2, p1 + q2, p1 + q1, p1)


def group_of(k):
    return 0 if k == 0 else 1 if k < 16 else 2 if k == 16 else 3 if k < 24 else 4


def cross_inverse(load_x, load_fx, load_s, load_fs, tw_ref, mat_ref, y_ref, z_ref, store):
    hs = []
    for w in range(NWIN):
        fx = [stack2(f) for f in load_fx(w)]
        hs.append(weights(load_fs(w), fx))
    for k in range(HALF):
        cr = ci = None
        for w in range(NWIN):
            xr, xi = [stack2(x) for x in load_x(w, k)]
            sr, si = load_s(w, k)
            h = hs[w][group_of(k)]
            tr = (sr * xr + si * xi) * h
            ti = (si * xr - sr * xi) * h
            cr = tr if cr is None else cr + tr
            ci = ti if ci is None else ci + ti
        put(y_ref, k, cr, ci)
    fast_dot(y_ref, mat_ref, z_ref)
    bins = []
    for k in range(HALF):
        re, im = z_ref[pl.ds(16 * k, 16), 0:128], z_ref[pl.ds(16 * k, 16), 128:256]
        c, s = stack2(tw_ref[k, 0]), stack2(tw_ref[k, 1])
        real = re * c - im * s
        bins.append((V(real), None if k in (0, 24) else V(re * s + im * c)))
    for j, x in enumerate(slow_inverse(bins)):
        store(j, x.get())
EARLY = 8
SLOTS = 3
GROUP = 16
LINE = 8
PIECE = NFFT // GROUP
CHUNKS = ((0, 16), (16, 16), (32, 8))
MESH = pl.DeviceIdType.MESH


def gather_kernel(ids_hbm, x_ref, flat_ref, fw_hbm, tw_hbm, iv_hbm, it_hbm, xs, fx, ss, fs, iv_ref, it_ref, early,
                  ids_ref, fw_ref, tw_ref, y, z, flat, recvx, part, recv1, recv2, srcs,
                  load_sem, flat_sem, own_sem, send_x, recv_x, send1, got1, send2, got2, send3, got3):
    rec, ch = lax.axis_index("rec"), lax.axis_index("ch")
    q, x_hi = ch // 2, ch % 2
    line = x_hi * 4 + rec
    pair, core = rec // 2, rec % 2
    sibling = rec + 1 - 2 * (rec % 2)
    far = [(rec + 2) % 4, (sibling + 2) % 4]
    hops = lambda offset: sum(min(d, 4 - d) for d in offset)
    offsets = sorted(((a, b) for a in range(4) for b in range(4) if a or b), key=hops, reverse=True)
    q_peer = [(q // 4 + a) % 4 * 4 + (q % 4 + b) % 4 for a, b in offsets]
    q_id = [(rec, p * 2 + x_hi) for p in q_peer]
    l_peer = [(line // 2 + i) % 4 * 2 + (line + j) % 2 for i, j in ((2, 0), (2, 1), (1, 0), (3, 0), (1, 1), (3, 1), (0, 1))]
    l_id = [(p % 4, q * 2 + p // 4) for p in l_peer]

    load_ids = pltpu.make_async_copy(ids_hbm, ids_ref, load_sem.at[0])
    quarter = NFFT // 4
    load_flat = [pltpu.make_async_copy(flat_ref.at[:, pl.ds(quarter * j, quarter)], flat.at[j], flat_sem.at[j]) for j in range(4)]
    load_fw = pltpu.make_async_copy(fw_hbm, fw_ref, load_sem.at[1])
    load_tw = pltpu.make_async_copy(tw_hbm, tw_ref, load_sem.at[2])
    load_own = pltpu.make_async_copy(x_ref.at[rec], recvx.at[rec], own_sem)
    load_iv = pltpu.make_async_copy(iv_hbm, iv_ref, load_sem.at[3])
    load_it = pltpu.make_async_copy(it_hbm, it_ref, load_sem.at[4])
    load_ids.start()
    for m in load_flat:
        m.start()
    barrier = pltpu.get_barrier_semaphore()
    for d in q_id + l_id:
        pl.semaphore_signal(barrier, inc=1, device_id=d, device_id_type=MESH)

    def move_x(n, peer, start, rows):
        return pltpu.make_async_remote_copy(
            src_ref=x_ref.at[peer, pl.ds(start, rows), :], dst_ref=recvx.at[rec, pl.ds(start, rows), :],
            send_sem=send_x.at[n], recv_sem=recv_x.at[n], device_id=(peer, ch), device_id_type=MESH)

    moves = []
    for c, (start, rows) in enumerate(CHUNKS):
        moves.append([move_x(2 * c + i, far[i], start, rows) for i in range(2)])
    near = move_x(6, sibling, 0, 40)

    load_ids.wait()
    row = lax.broadcasted_iota(jnp.int32, (NSRC, 160), 0)
    col = lax.broadcasted_iota(jnp.int32, (NSRC, 160), 1)
    ids = jnp.zeros((NSRC, 160), jnp.int32)
    for s in range(NSRC):
        ids = jnp.where(row == s, ids_ref[s], ids)
    here = (col // 40) * 1280 + ch * 40 + col % 40
    chooser = jnp.where(ids == here, 1.0, 0.0).astype(jnp.bfloat16)
    for j in range(GROUP):
        if j % 4 == 0:
            load_flat[j // 4].wait()
        part[j] = jnp.dot(chooser, flat[j // 4, :, pl.ds(PIECE * (j % 4), PIECE)], preferred_element_type=jnp.float32)
    recv1[q] = part[q]

    pl.semaphore_wait(barrier, GROUP - 1 + LINE - 1)
    moves[0][0].start()
    step1 = [pltpu.make_async_remote_copy(
        src_ref=part.at[p], dst_ref=recv1.at[q], send_sem=send1.at[i], recv_sem=got1.at[i],
        device_id=d, device_id_type=MESH) for i, (p, d) in enumerate(zip(q_peer, q_id))]
    for m in step1:
        m.start()
    near.start()
    for m in (load_fw, load_tw, load_own, load_iv, load_it):
        m.start()

    def whole_block(w, p):
        rows = pl.ds(pl.multiple_of(16 * p, 16), 16)
        forward16(lambda n: recvx[w, rows, pl.ds(FAST * n, FAST)].astype(jnp.float32), tw_ref, fw_ref, y, xs.at[2 * w + p])
        f = factors(xs.at[2 * w + p])
        for half in range(2):
            for i in range(4):
                fx[w, 2 * p + half, i] = f[i][8 * half : 8 * half + 8, :]

    def half_block(first):
        def load(n):
            return jnp.concatenate(
                [recvx[first + half, pl.ds(32, 8), pl.ds(FAST * n, FAST)].astype(jnp.float32) for half in range(2)], axis=0)

        block = 8 + first // 2
        forward16(load, tw_ref, fw_ref, y, xs.at[block])
        f = factors(xs.at[block])
        for half in range(2):
            for i in range(4):
                fx[first + half, 4, i] = f[i][8 * half : 8 * half + 8, :]

    for m in (load_fw, load_tw, load_own, load_iv, load_it):
        m.wait()

    def own(p, _):
        whole_block(rec, p)
        return 0

    lax.fori_loop(0, 2, own, 0)

    for m in step1:
        m.wait_recv()
    total = recv1[0]
    for j in range(1, GROUP):
        total = total + recv1[j]
    recv2[line] = total
    step2 = [pltpu.make_async_remote_copy(
        src_ref=recv2.at[line], dst_ref=recv2.at[line], send_sem=send2.at[i], recv_sem=got2.at[i],
        device_id=d, device_id_type=MESH) for i, d in enumerate(l_id)]
    for m in step2 + moves[0][1:] + moves[1] + moves[2]:
        m.start()

    near.wait_recv()

    def second(p, _):
        whole_block(sibling, p)
        return 0

    lax.fori_loop(0, 2, second, 0)

    for m in step2:
        m.wait_recv()
    srcs[core, q] = jnp.concatenate(
        [recv2[2 * core + i] + recv2[4 + 2 * core + i] for i in range(2)], axis=0).astype(jnp.bfloat16)
    step3 = [pltpu.make_async_remote_copy(
        src_ref=srcs.at[core, q], dst_ref=srcs.at[core, q], send_sem=send3.at[i], recv_sem=got3.at[i],
        device_id=d, device_id_type=MESH) for i, d in enumerate(q_id)]
    for m in step3:
        m.start()
    half_block(2 * pair)

    def far_chunk(n):
        for m in moves[n]:
            m.wait_recv()

        def two(i, _):
            whole_block(2 * (1 - pair) + i, n)
            return 0

        lax.fori_loop(0, 2, two, 0)

    far_chunk(0)
    for m in step3:
        m.wait_recv()

    share = pltpu.make_async_remote_copy(
        src_ref=srcs.at[core], dst_ref=srcs.at[core], send_sem=send_x.at[7], recv_sem=recv_x.at[7],
        device_id=(sibling, ch), device_id_type=MESH)
    share.start()

    def source_block(i, _):
        p = (core + i) % 2

        @pl.when(i == 1)
        def _():
            share.wait_recv()

        def load(n):
            return srcs[p, n // 3, :, pl.ds(FAST * (n % 3), FAST)].astype(jnp.float32)

        forward16(load, tw_ref, fw_ref, y, z)
        f = factors(z)
        for half in range(2):
            w = 2 * p + half
            for s in range(NSRC):
                r = 8 * half + s
                for i in range(4):
                    fs[w, s // 2, i, pl.ds(8 * (s % 2), 8), :] = jnp.broadcast_to(f[i][r : r + 1, :], (8, FAST))
                for k in range(HALF):
                    ss[w, s // 2, k, pl.ds(8 * (s % 2), 8), :] = jnp.broadcast_to(z[pl.ds(16 * k + r, 1), :], (8, 256))
        return 0

    lax.fori_loop(0, 2, source_block, 0)

    def unit(u, _):
        cb, sp = u // 4, u % 4

        def store(j, x):
            for half in range(2):
                early[2 * sp + half, pl.ds(pl.multiple_of(8 * cb, 8), 8), pl.ds(FAST * j, FAST)] = x[8 * half : 8 * half + 8]

        correlate_unit(cb, sp, xs, fx, ss, fs, it_ref, iv_ref, y, z, store)
        return 0

    lax.fori_loop(0, EARLY, unit, 0)
    far_chunk(1)
    for m in moves[2]:
        m.wait_recv()
    half_block(2 * (1 - pair))
    for m in step1 + step2 + step3 + moves[0] + moves[1] + moves[2] + [near, share]:
        m.wait_send()


def correlate_unit(cb, sp, xs, fx, ss, fs, tw_ref, iv_ref, y, z, store):
    def load_x(w, k):
        block = jnp.where(cb < 4, 2 * w + cb // 2, 8 + w // 2)
        rows = pl.ds(pl.multiple_of(16 * k + 8 * jnp.where(cb < 4, cb % 2, w % 2), 8), 8)
        return xs[block, rows, 0:128], xs[block, rows, 128:256]

    cross_inverse(
        load_x,
        lambda w: [fx[w, cb, i] for i in range(4)],
        lambda w, k: (ss[w, sp, k, :, 0:128], ss[w, sp, k, :, 128:256]),
        lambda w: [fs[w, sp, i] for i in range(4)],
        tw_ref, iv_ref, y, z, store)


def correlate_kernel(xs, fx, ss, fs, iv_ref, tw_ref, early, out_ref, y, z, obuf, osem, early_sem):
    rows = 2 * EARLY
    copies = [pltpu.make_async_copy(early.at[s], out_ref.at[s, pl.ds(0, rows), :], early_sem.at[s]) for s in range(NSRC)]
    for m in copies:
        m.start()

    def send(slot, cb, sp):
        return [pltpu.make_async_copy(
            obuf.at[slot, half],
            out_ref.at[2 * sp + half, pl.ds(pl.multiple_of(8 * cb, 8), 8), :],
            osem.at[slot, half]) for half in range(2)]

    def unit(u, _):
        cb, sp = u // 4, u % 4
        slot = u % SLOTS

        @pl.when(u >= EARLY + SLOTS)
        def _():
            for m in send(slot, (u - SLOTS) // 4, (u - SLOTS) % 4):
                m.wait()

        def store(j, x):
            for half in range(2):
                obuf[slot, half, :, pl.ds(FAST * j, FAST)] = x[8 * half : 8 * half + 8]

        correlate_unit(cb, sp, xs, fx, ss, fs, tw_ref, iv_ref, y, z, store)
        for m in send(slot, cb, sp):
            m.start()
        return 0

    lax.fori_loop(EARLY, 20, unit, 0)
    for u in range(20 - SLOTS, 20):
        for m in send(u % SLOTS, u // 4, u % 4):
            m.wait()
    for m in copies:
        m.wait()


def correlate(spectra, iv, tw, early):
    channels = 8 * spectra[1].shape[1]
    vmem = pl.BlockSpec(memory_space=pltpu.VMEM)
    hbm = pl.BlockSpec(memory_space=pltpu.HBM)
    f32, dma = jnp.float32, pltpu.SemaphoreType.DMA
    return pl.pallas_call(
        correlate_kernel,
        out_shape=jax.ShapeDtypeStruct((NSRC, channels, NFFT), f32),
        in_specs=[vmem] * 7,
        out_specs=hbm,
        scratch_shapes=[
            pltpu.VMEM((ROWS, 256), f32),
            pltpu.VMEM((ROWS, 256), f32),
            pltpu.VMEM((SLOTS, 2, 8, NFFT), f32),
            dma((SLOTS, 2)),
            dma((NSRC,)),
        ],
        compiler_params=pltpu.CompilerParams(vmem_limit_bytes=32 * 2**20),
    )(*spectra, iv, tw, early)


def shards(samples, source_ids):
    fw, iv, tw = tables()
    channels = samples.shape[2]
    vmem = pl.BlockSpec(memory_space=pltpu.VMEM)
    hbm = pl.BlockSpec(memory_space=pltpu.HBM)
    f32, bf16 = jnp.float32, jnp.bfloat16
    dma = pltpu.SemaphoreType.DMA
    twist, square = pltpu.VMEM((HALF, 2, 8, FAST), f32), pltpu.VMEM((512, 256), bf16)
    spectra = pl.pallas_call(
        gather_kernel,
        out_shape=[
            jax.ShapeDtypeStruct((12, ROWS, 256), f32),
            jax.ShapeDtypeStruct((NWIN, 5, 4, 8, FAST), f32),
            jax.ShapeDtypeStruct((NWIN, 4, HALF, 16, 256), f32),
            jax.ShapeDtypeStruct((NWIN, 4, 4, 16, FAST), f32),
            jax.ShapeDtypeStruct((512, 256), bf16),
            jax.ShapeDtypeStruct((HALF, 2, 8, FAST), f32),
            jax.ShapeDtypeStruct((NSRC, 2 * EARLY, NFFT), f32),
        ],
        in_specs=[hbm] * 7,
        out_specs=[vmem] * 7,
        scratch_shapes=[
            pltpu.SMEM((NSRC,), jnp.int32),
            square,
            twist,
            pltpu.VMEM((ROWS, 256), f32),
            pltpu.VMEM((ROWS, 256), f32),
            pltpu.VMEM((4, 4 * channels, NFFT // 4), bf16),
            pltpu.VMEM((NWIN, channels, NFFT), bf16),
            pltpu.VMEM((GROUP, NSRC, PIECE), f32),
            pltpu.VMEM((GROUP, NSRC, PIECE), f32),
            pltpu.VMEM((LINE, NSRC, PIECE), f32),
            pltpu.VMEM((2, GROUP, 2 * NSRC, PIECE), bf16),
            dma((5,)), dma((4,)), dma, dma((8,)), dma((8,)), dma((15,)), dma((15,)), dma((7,)), dma((7,)), dma((15,)), dma((15,)),
        ],
        compiler_params=pltpu.CompilerParams(
            collective_id=0, has_side_effects=True, vmem_limit_bytes=32 * 2**20),
    )(*[pltpu.with_memory_space_constraint(jnp.asarray(a), pltpu.HBM) for a in (
        source_ids, samples[0], samples.reshape(4 * channels, NFFT), fw, tw[:, 0:2], iv, tw[:, 2:4])])
    return correlate(spectra[0:4], *spectra[4:7])


def solution(mesh):
    return jax.shard_map(
        shards,
        mesh=mesh,
        in_specs=(P("rec", None, "ch", None), P()),
        out_specs=P(None, ("rec", "ch"), None),
        check_vma=False,
    )
```
